512 devices in a mesh: group: 64 (over z_hi, y, core), tp: 8 (over z_lo, x).
Axes of the slice: x: 4, y: 8, z: 8 (z_hi: 4, z_lo: 2; z = z_hi * 2 + z_lo), core: 2. Of those that a mesh axis runs over, the one named last changes fastest.
Arguments:
- hidden: bfloat16 [2, 4096, 8192], P(None, 'group', 'tp'), may hold values from -6 to 6
- queries: bfloat16 [2, 4096, 8, 512], P(None, 'group', 'tp'), may hold values from -16 to 16
- kv_cache: bfloat16 [4096, 8, 64, 256], P('group', 'tp'), may hold values from -16 to 16
- lengths: int32 [4096], P('group'), may hold values from 2 to 128, as said below
- weights: bfloat16 [64, 8192, 1024], P('group', None, 'tp'), may hold values from -0.0625 to 0.0625
- kv_bias: bfloat16 [64, 1024], P('group', 'tp'), may hold values from -3 to 3
- owner_group: int32 [1], replicated, may hold values from 0 to 63
Outputs:
- attended: bfloat16 [2, 4096, 4096], P(None, 'group', 'tp')
The draws below stay inside these ranges and needn't reach their ends.
Inputs may be any that keep to these rules, and one draw needn't show every extreme that they name: `lengths`: some row holds exactly 128 cached tokens.
All inputs are finite; a program needn't handle non-finite values.
Results may differ from the reference program's by a relative error of at most 0.0043.
Values may be sent and summed in bfloat16 or wider, within the bound.
A program may use at most 64 MiB of HBM per device.

```python
import math
import jax
import jax.numpy as jnp
from jax import lax

D = 8192
HD = 128
KVH = 4
QPK = 8
RG = 64
CACHE = 128
QH = 32
KV = 1024
CH = 64
ROWS = 4096
N_GROUP = 64


def draw_queries(key, part):
    shape_all = (2, ROWS, 2 * KVH, 4 * HD)
    values = jnp.clip(jax.random.normal(jax.random.fold_in(key, 1), shape_all), -6.0, 6.0)
    return values.astype(jnp.bfloat16)


def draw_kv_cache(key, part):
    shape_all = (ROWS, 2 * KVH, CH, 2 * HD)
    values = jnp.clip(jax.random.normal(jax.random.fold_in(key, 3), shape_all), -6.0, 6.0)
    return values.astype(jnp.bfloat16)


def draw_lengths(key, part):
    values = jax.random.randint(jax.random.fold_in(key, 5), (ROWS,), 2, CACHE + 1)
    picked = jax.random.randint(jax.random.fold_in(key, 6), (), 0, ROWS)
    return values.at[picked].set(CACHE).astype(jnp.int32)


def block_levels(stream_key, extent, split, low, high):
    def one(position, shards_of):
        heights = jax.random.uniform(jax.random.fold_in(jax.random.fold_in(stream_key, 6), position), (shards_of,), jnp.float32, low / len(split), high / len(split))
        return jnp.repeat(jnp.exp(heights), extent[position] // shards_of).reshape((-1,) + (1,) * (len(extent) - position - 1))

    level = one(*split[0])
    for cut in split[1:]:
        level = level * one(*cut)
    return level


def scatter_about(rng, dims, scale, limit, split=(), kind=jnp.bfloat16):
    values = scale * jax.random.normal(rng, dims, jnp.float32)
    if split:
        values = values * block_levels(rng, dims, split, -0.22, 0.18)
    return jnp.clip(values, -limit, limit).astype(kind)


def setup_inputs(seed: int = 0) -> dict:
    arg_keys = jax.random.split(jax.random.key(seed), 8)
    return {
        "hidden": scatter_about(arg_keys[0], (2, ROWS, D), 1.0, 6.0, ((1, 64), (2, 8))),
        "queries": draw_queries(jax.random.fold_in(arg_keys[7], 71), 0),
        "kv_cache": draw_kv_cache(jax.random.fold_in(arg_keys[7], 71), 0),
        "lengths": draw_lengths(jax.random.fold_in(arg_keys[7], 71), 0),
        "weights": scatter_about(arg_keys[4], (N_GROUP, D, KV), D ** -0.5, 0.0625, ((0, 64), (2, 8))),
        "kv_bias": scatter_about(arg_keys[5], (N_GROUP, KV), 0.5, 3.0, ((0, 64), (1, 8))),
        "owner_group": jax.random.randint(arg_keys[6], (1,), 0, N_GROUP).astype(jnp.int32),
    }


def rotate(key_part, positions):
    head_width = key_part.shape[-1]
    half_width = head_width // 2
    freq = jnp.exp(-(jnp.arange(half_width, dtype=jnp.float32) * (2.0 / head_width)) * math.log(1000000.0))
    angle = positions[:, None, None] * freq[None, None, :]
    cosine = jnp.cos(angle)
    sine = jnp.sin(angle)
    first_half = key_part[..., :half_width]
    second_half = key_part[..., half_width:]
    return jnp.concatenate([first_half * cosine - second_half * sine, second_half * cosine + first_half * sine], -1)

def split_partials(query_heads, cache_part, start_pos, row_lengths, new_keys, new_values):
    head_width = query_heads.shape[-1]
    score_scale = 1.0 / math.sqrt(head_width)
    positions_count = cache_part.shape[2]
    key_part = cache_part[..., :head_width].astype(jnp.float32)
    value_part = cache_part[..., head_width:].astype(jnp.float32)
    query_f = query_heads.astype(jnp.float32)
    scores = jnp.einsum('rhqd,rhcd->rhqc', query_f, key_part) * score_scale
    usable = (start_pos + jnp.arange(positions_count, dtype=jnp.int32))[None, :] < row_lengths[:, None]
    usable = jnp.broadcast_to(usable[:, None, None, :], scores.shape)
    if new_keys is not None:
        new_scores = jnp.einsum('rhqd,rhnd->rhqn', query_f, new_keys.astype(jnp.float32)) * score_scale
        scores = jnp.concatenate([scores, new_scores], -1)
        usable = jnp.concatenate([usable, jnp.ones(new_scores.shape, dtype=bool)], -1)
        value_part = jnp.concatenate([value_part, new_values.astype(jnp.float32)], 2)
    peak_score = lax.optimization_barrier(jnp.max(jnp.where(usable, scores, -1e+30), -1))
    raw_weights = jnp.where(usable, jnp.exp(scores - peak_score[..., None]), 0.0)
    summed = lax.optimization_barrier(jnp.sum(raw_weights, -1))
    rounded = lax.optimization_barrier(raw_weights.astype(jnp.bfloat16))
    weighted = jnp.einsum('rhqc,rhcd->rhqd', rounded.astype(jnp.float32), value_part)
    return (weighted, peak_score, summed)

def merge_splits(first_split, second_split):
    peak_score = jnp.maximum(first_split[1], second_split[1])
    first_scale = jnp.exp(first_split[1] - peak_score)
    second_scale = jnp.exp(second_split[1] - peak_score)
    top_part = first_split[0] * first_scale[..., None] + second_split[0] * second_scale[..., None]
    bottom_part = first_split[2] * first_scale + second_split[2] * second_scale
    return top_part / bottom_part[..., None]

def reference(hidden, queries, kv_cache, lengths, weights, kv_bias, owner_group):
    fresh_weights = lax.dynamic_index_in_dim(weights, owner_group[0], 0, keepdims=False)
    fresh_bias = lax.dynamic_index_in_dim(kv_bias, owner_group[0], 0, keepdims=False)

    def project(rows_in, matrix, bias_row, positions):
        summed = jnp.dot(rows_in, matrix, preferred_element_type=jnp.float32) + bias_row.astype(jnp.float32)[None, :]
        summed = summed.reshape(RG, 2, KVH, HD)
        new_key = rotate(summed[:, 0], positions).astype(jnp.bfloat16)
        new_value = summed[:, 1].astype(jnp.bfloat16)
        return (new_key, new_value)

    def one_group(items):
        first_rows, second_rows, group_queries, group_cache, group_lengths, own_weights, own_bias = items
        positions = group_lengths.astype(jnp.float32)
        key_first, value_first = project(first_rows, own_weights, own_bias, positions)
        key_second, value_second = project(second_rows, fresh_weights, fresh_bias, positions + 1.0)
        halves = group_cache.reshape(RG, 2, KVH, CH, 2 * HD)
        step_news = [(key_first[:, :, None], value_first[:, :, None]), (jnp.stack([key_first, key_second], 2), jnp.stack([value_first, value_second], 2))]
        results = []
        for step_index in range(2):
            query_heads = group_queries[step_index].reshape(RG, 2, KVH, 4, HD)
            query_heads = jnp.transpose(query_heads, (0, 2, 1, 3, 4)).reshape(RG, KVH, QPK, HD)
            first_split = split_partials(query_heads, halves[:, 0], 0, group_lengths, step_news[step_index][0], step_news[step_index][1])
            second_split = split_partials(query_heads, halves[:, 1], CH, group_lengths, None, None)
            merged = merge_splits(first_split, second_split)
            merged = jnp.transpose(merged.reshape(RG, KVH, 2, 4, HD), (0, 2, 1, 3, 4))
            results.append(merged.reshape(RG, QH * HD).astype(jnp.bfloat16))
        return jnp.stack(results)
    items = (hidden[0].reshape(N_GROUP, RG, D), hidden[1].reshape(N_GROUP, RG, D), jnp.transpose(queries.reshape(2, N_GROUP, RG, 2 * KVH, 4 * HD), (1, 0, 2, 3, 4)), kv_cache.reshape(N_GROUP, RG, 2 * KVH, CH, 2 * HD), lengths.reshape(N_GROUP, RG), weights, kv_bias)
    outputs = lax.map(one_group, items)
    return jnp.transpose(outputs, (1, 0, 2, 3)).reshape(2, ROWS, QH * HD)
```

```python
import functools
import math

import jax
import jax.numpy as jnp
from jax import lax
from jax.experimental import pallas as pl
from jax.experimental.pallas import tpu as pltpu
from jax.sharding import PartitionSpec as P

MESH = pl.DeviceIdType.MESH
BF16 = jnp.bfloat16
F32 = jnp.float32
NEG = -1e30
NY, NZ, NX = 8, 4, 4
LONG, SHORT = 4, 3
ROWS, D, HD, HALF, CHUNK, QUART = 64, 8192, 128, 4096, 512, 128
SCALE2 = math.log2(math.e) / math.sqrt(128.0)


def remote(src, dst, send_sem, recv_sem, device):
    return pltpu.make_async_remote_copy(
        src_ref=src, dst_ref=dst, send_sem=send_sem, recv_sem=recv_sem,
        device_id=device, device_id_type=MESH,
    )


def dot_t(a, b):
    return lax.dot_general(a, b, (((1,), (1,)), ((), ())), preferred_element_type=F32)


def kernel(
    w_hbm, kv_hbm, hid_hbm, q_hbm, len_ref, bias_ref, owner_ref, out_ref,
    wv, xbuf, rl, rs, zr, wf, hf, kvv, qo, qp,
    oo, mo, lo, po, pml, ro, rml, lenc, cosf, sinf,
    bias_mine, bias_die, bias_chip, bias_y, bias_row, bias_z,
    kvown, kvpeer, acc,
    loc_sem, die_s, die_r, rl_s, rl_r, rs_s, rs_r, z_s, z_r, zg_s, zg_r,
    al_s, al_r, as_s, as_r, df_s, df_r,
    hz_s, hz_r, hx_s, hx_r, q_s, q_r, p_s, p_r, e_s, e_r,
    bd_s, bd_r, by_s, by_r, bz_s, bz_r,
):
    group = lax.axis_index("group")
    tp = lax.axis_index("tp")
    core = group % 2
    y = (group // 2) % NY
    zh = group // (2 * NY)
    x = tp % NX
    zl = tp // NX
    step_l = 1 - 2 * core

    def at(zz, yy, cc):
        return (zz * (2 * NY) + yy * 2 + cc, tp)

    def wrap_y(v):
        return (v + 4 * NY) % NY

    sibling = at(zh, y, 1 - core)
    ahead = at(zh, wrap_y(y + step_l), core)
    behind = at(zh, wrap_y(y - step_l), core)
    z_peers = [at((zh + j) % NZ, y, core) for j in range(1, NZ)]
    y_peers = [at(zh, (y + j) % NY, core) for j in range(1, NY)]
    partner_tp = (tp + NX) % (2 * NX)
    partner = (group, partner_tp)
    x_peers = [(group, zl * NX + (x + j) % NX) for j in range(1, NX)]

    kv_copy = pltpu.make_async_copy(kv_hbm, kvv, loc_sem.at[0])
    w_copy = pltpu.make_async_copy(w_hbm, wv, loc_sem.at[1])
    h_copy = pltpu.make_async_copy(hid_hbm, hf.at[:, tp], loc_sem.at[2])
    q_copy = pltpu.make_async_copy(q_hbm, qo, loc_sem.at[3])
    w_copy.start()
    q_copy.start()
    h_copy.start()
    kv_copy.start()

    barrier = pltpu.get_barrier_semaphore()
    everyone = [sibling, partner] + x_peers + z_peers + y_peers
    for other in everyone:
        pl.semaphore_signal(barrier, inc=1, device_id=other, device_id_type=MESH)
    pl.semaphore_wait(barrier, len(everyone))

    order = []
    for s in range(LONG):
        order.append(wrap_y(y + step_l * (LONG - s)))
        if s < SHORT:
            order.append(wrap_y(y - step_l * (SHORT - s)))
    order.append(y)

    def rows_of(chunk, quarter=None):
        if quarter is None:
            return pl.ds(pl.multiple_of(chunk * CHUNK, CHUNK), CHUNK)
        return pl.ds(pl.multiple_of(chunk * CHUNK + quarter * QUART, QUART), QUART)

    def half_rows(half, chunk, quarter=None):
        if quarter is None:
            return pl.ds(pl.multiple_of(half * HALF + chunk * CHUNK, CHUNK), CHUNK)
        return pl.ds(pl.multiple_of(half * HALF + chunk * CHUNK + quarter * QUART, QUART), QUART)

    die = []
    for n in range(NY):
        if n == NY - 1:
            chunk = y
        elif n % 2 == 0:
            chunk = wrap_y(y - step_l * (LONG - n // 2))
        else:
            chunk = wrap_y(y + step_l * (SHORT - n // 2))
        die.append(remote(
            w_hbm.at[half_rows(1 - core, chunk)], xbuf.at[rows_of(chunk)],
            die_s.at[n], die_r.at[n], sibling))
        die[-1].start()

    q_send = remote(q_hbm, qp, q_s, q_r, partner)
    q_send.start()
    hz, hx = {}, {}
    for s in (1, 0):
        hz[s] = remote(hid_hbm.at[s], hf.at[s, tp], hz_s.at[s], hz_r.at[s], partner)
        hz[s].start()
        for j in range(NX - 1):
            hx[s, 0, j] = remote(
                hid_hbm.at[s], hf.at[s, tp], hx_s.at[s, 0, j], hx_r.at[s, 0, j], x_peers[j])
            hx[s, 0, j].start()

    owner = owner_ref[0]
    mine_w = jnp.full((1, HD), (owner == group).astype(F32)).astype(BF16)
    sib_w = jnp.full((1, HD), (owner == group + 1 - 2 * core).astype(F32)).astype(BF16)

    bias_mine[...] = jnp.broadcast_to(bias_ref[...] * mine_w, (16, HD))
    b_die = remote(bias_mine, bias_die, bd_s, bd_r, sibling)
    b_die.start()

    w_copy.wait()

    def combine(n):
        chunk = order[n]
        die[n].wait_recv()
        at_rows = rows_of(chunk)
        xbuf[at_rows] = wv[half_rows(core, chunk)] * mine_w + xbuf[at_rows] * sib_w

    long_send, short_send = {}, {}

    def reduce_step(s):
        chunk = wrap_y(y + step_l * (LONG - s))
        for q in range(4):
            part = pl.ds(q * QUART, QUART)
            if s == 0:
                src = xbuf.at[rows_of(chunk, q)]
            else:
                long_send[s - 1, q].wait_recv()
                rl[s - 1, part] = rl[s - 1, part] + xbuf[rows_of(chunk, q)]
                src = rl.at[s - 1, part]
            long_send[s, q] = remote(src, rl.at[s, part], rl_s.at[s, q], rl_r.at[s, q], ahead)
            long_send[s, q].start()
            if s < SHORT:
                other = wrap_y(y - step_l * (SHORT - s))
                if s == 0:
                    src = xbuf.at[rows_of(other, q)]
                else:
                    short_send[s - 1, q].wait_recv()
                    rs[s - 1, part] = rs[s - 1, part] + xbuf[rows_of(other, q)]
                    src = rs.at[s - 1, part]
                short_send[s, q] = remote(
                    src, rs.at[s, part], rs_s.at[s, q], rs_r.at[s, q], behind)
                short_send[s, q].start()

    combine(0)
    combine(1)
    reduce_step(0)
    for n in range(2, NY):
        combine(n)

    lens = jnp.broadcast_to(len_ref[...].astype(F32), (ROWS, ROWS))
    diag = lax.broadcasted_iota(jnp.int32, (ROWS, ROWS), 0) == lax.broadcasted_iota(
        jnp.int32, (ROWS, ROWS), 1)
    len_col = jnp.sum(jnp.where(diag, lens, 0.0), axis=1, keepdims=True)
    lenc[...] = jnp.broadcast_to(len_col, (ROWS, HD))

    def attend(block):
        kept = []
        for sub in range(2):
            r0 = block * 16 + sub * 8
            pieces = []
            for src in (qo, qp):
                for s in range(2):
                    for j in range(4):
                        part = src[s, pl.ds(block * 16, 16), pl.ds(j * HD, HD)].astype(F32)
                        pieces.append(part[sub * 8:sub * 8 + 8])
            lhs = jnp.concatenate(pieces, axis=0).astype(BF16)
            cache = pl.ds(r0 * 64, 512)
            scores = dot_t(lhs, kvv[cache, pl.ds(0, HD)]).reshape(16, 8, 512)
            row_id = lax.broadcasted_iota(jnp.int32, (8, 512), 0)
            col_id = lax.broadcasted_iota(jnp.int32, (8, 512), 1)
            length = lenc[pl.ds(r0, 8), :][:, :1]
            pos = (col_id % 64 + zl * 64).astype(F32)
            usable = jnp.logical_and(col_id // 64 == row_id, pos < length)[None]
            peak = jnp.max(jnp.where(usable, scores, NEG), axis=2, keepdims=True)
            weight = jnp.exp2(jnp.where(usable, (scores - peak) * SCALE2, NEG))
            total = jnp.sum(weight, axis=2, keepdims=True)
            weighted = jnp.dot(
                weight.astype(BF16).reshape(128, 512), kvv[cache, pl.ds(HD, HD)],
                preferred_element_type=F32).reshape(16, 8, HD)
            rows = pl.ds(r0, 8)
            oo[:, rows] = weighted[:8]
            mo[:, rows] = jnp.broadcast_to(peak[:8], (8, 8, HD))
            lo[:, rows] = jnp.broadcast_to(total[:8], (8, 8, HD))
            kept.append(weighted[8:])
            lane = lax.broadcasted_iota(jnp.int32, (8, HD), 1)
            packed = jnp.zeros((8, HD), F32)
            for i in range(8):
                packed = jnp.where(lane == i, peak[8 + i], packed)
                packed = jnp.where(lane == 8 + i, total[8 + i], packed)
            pml[rows] = packed
        po[:, pl.ds(block * 16, 16)] = jnp.concatenate(kept, axis=1).astype(BF16)

    q_copy.wait()
    kv_copy.wait()
    b_die.wait_recv()
    bias_chip[...] = bias_mine[...] + bias_die[...]
    b_y = [remote(bias_chip, bias_y.at[j], by_s.at[j], by_r.at[j], y_peers[j]) for j in range(NY - 1)]
    for copy in b_y:
        copy.start()
    q_send.wait_recv()
    attend(0)

    reduce_step(1)

    for s in (1, 0):
        hz[s].wait_recv()
        for j in range(NX - 1):
            hx[s, 1, j] = remote(
                hf.at[s, partner_tp], hf.at[s, partner_tp], hx_s.at[s, 1, j], hx_r.at[s, 1, j],
                x_peers[j])
            hx[s, 1, j].start()
    attend(1)

    reduce_step(2)
    attend(2)
    for copy in b_y:
        copy.wait_recv()
    total_bias = bias_chip[...]
    for j in range(NY - 1):
        total_bias = total_bias + bias_y[j]
    bias_row[...] = total_bias
    b_z = [remote(bias_row, bias_z.at[j], bz_s.at[j], bz_r.at[j], z_peers[j]) for j in range(NZ - 1)]
    for copy in b_z:
        copy.start()

    reduce_step(3)
    attend(3)
    p_send = [
        remote(po, ro, p_s.at[0], p_r.at[0], partner),
        remote(pml, rml, p_s.at[1], p_r.at[1], partner),
    ]
    for copy in p_send:
        copy.start()

    for q in range(4):
        part = pl.ds(q * QUART, QUART)
        long_send[LONG - 1, q].wait_recv()
        short_send[SHORT - 1, q].wait_recv()
        rl[LONG - 1, part] = rl[LONG - 1, part] + rs[SHORT - 1, part] + xbuf[rows_of(y, q)]
    z_send = []
    for j in range(NZ - 1):
        part = pl.ds(pl.multiple_of((zh + j + 1) % NZ * QUART, QUART), QUART)
        z_send.append(remote(rl.at[LONG - 1, part], zr.at[j], z_s.at[j], z_r.at[j], z_peers[j]))
        z_send[-1].start()

    lane = lax.broadcasted_iota(jnp.int32, (ROWS, HD), 1)
    freq = jnp.exp(-((lane % 64).astype(F32) * (2.0 / HD)) * math.log(1000000.0))
    is_key = tp < NX
    for s in range(2):
        angle = (lenc[...] + float(s)) * freq
        sine = jnp.sin(angle)
        cosf[s] = jnp.where(is_key, jnp.cos(angle), 1.0)
        sinf[s] = jnp.where(is_key, jnp.where(lane < 64, -sine, sine), 0.0)

    own_part = pl.ds(pl.multiple_of(zh * QUART, QUART), QUART)
    total_w = rl[LONG - 1, own_part]
    for j in range(NZ - 1):
        z_send[j].wait_recv()
        total_w = total_w + zr[j]
    own_rows = half_rows(core, y, zh)
    wf[own_rows] = total_w
    zg = []
    for j in range(NZ - 1):
        zg.append(remote(wf.at[own_rows], wf.at[own_rows], zg_s.at[j], zg_r.at[j], z_peers[j]))
        zg[-1].start()

    al, ash, df = {}, {}, {}

    def forward(kind, s, i, chunk):
        rows = half_rows(core, chunk, (zh - i + NZ) % NZ)
        ref = wf.at[rows]
        if kind in ("own", "long") and s < LONG:
            al[s, i] = remote(ref, ref, al_s.at[s, i], al_r.at[s, i], ahead)
            al[s, i].start()
        if kind in ("own", "short") and s < SHORT:
            ash[s, i] = remote(ref, ref, as_s.at[s, i], as_r.at[s, i], behind)
            ash[s, i].start()
        n = 0 if kind == "own" else (s if kind == "long" else LONG + s)
        df[n, i] = remote(ref, ref, df_s.at[n, i], df_r.at[n, i], sibling)
        df[n, i].start()

    forward("own", 0, 0, y)
    for i in range(1, 4):
        zg[i - 1].wait_recv()
        forward("own", 0, i, y)

    def multiply(step, weights, half, chunk):
        block = half * NY + chunk
        feats = hf[step, block // 2, :, pl.ds(pl.multiple_of((block % 2) * CHUNK, CHUNK), CHUNK)]
        return jnp.dot(feats, weights[half_rows(half, chunk)], preferred_element_type=F32)

    def wait_features(s):
        for kind in range(2):
            for j in range(NX - 1):
                hx[s, kind, j].wait_recv()

    def from_sibling(n, chunk):
        for i in range(4):
            df[n, i].wait_recv()
        acc[...] += multiply(1, wf, 1 - core, chunk)

    def entry(s, total, bias):
        total = total + bias
        turned = total * cosf[s] + pltpu.roll(total, 64, 1) * sinf[s]
        kvown[s] = turned.astype(BF16)
        send = remote(kvown.at[s], kvpeer.at[s], e_s.at[s], e_r.at[s], partner)
        send.start()
        return send

    def add_entry(s, i, query, key, value):
        score = jnp.sum(query * key, axis=1, keepdims=True)
        old = mo[i]
        peak = jnp.maximum(old, score)
        keep = jnp.exp2((old - peak) * SCALE2)
        weight = jnp.exp2((score - peak) * SCALE2)
        return (
            peak,
            lo[i] * keep + weight,
            oo[i] * keep + weight.astype(BF16).astype(F32) * value,
        )

    def new_pair(s):
        own, other = kvown[s].astype(F32), kvpeer[s].astype(F32)
        return jnp.where(is_key, own, other), jnp.where(is_key, other, own)

    h_copy.wait()
    for s in range(1, LONG + 1):
        long_chunk = wrap_y(y - step_l * s)
        short_chunk = wrap_y(y + step_l * s)
        for i in range(4):
            al[s - 1, i].wait_recv()
            forward("long", s, i, long_chunk)
            if s <= SHORT:
                ash[s - 1, i].wait_recv()
                forward("short", s, i, short_chunk)
        if s == 1:
            wait_features(1)
            acc[...] = multiply(1, wf, core, y)
            from_sibling(0, y)
        else:
            from_sibling(s - 1, wrap_y(y + step_l * (s - 1)))
            from_sibling(LONG + s - 1, wrap_y(y - step_l * (s - 1)))
        acc[...] += multiply(1, wf, core, long_chunk)
        if s <= SHORT:
            acc[...] += multiply(1, wf, core, short_chunk)
        if s == 1:
            for copy in p_send:
                copy.wait_recv()
            for i in range(8):
                m2 = rml[:, i:i + 1]
                l2 = rml[:, 8 + i:9 + i]
                m1 = mo[i]
                peak = jnp.maximum(m1, m2)
                e1 = jnp.exp2((m1 - peak) * SCALE2)
                e2 = jnp.exp2((m2 - peak) * SCALE2)
                mo[i] = peak
                lo[i] = lo[i] * e1 + l2 * e2
                oo[i] = oo[i] * e1 + ro[i].astype(F32) * e2
        if s == 2:
            wait_features(0)
            total = jnp.zeros((ROWS, HD), F32)
            for t in range(8):
                total = total + jnp.dot(
                    hf[0, t], wv[t * 1024:(t + 1) * 1024], preferred_element_type=F32)
            e_send = [entry(0, total, bias_ref[...].astype(F32))]
        if s == 3:
            e_send[0].wait_recv()
            key, value = new_pair(0)
            for i in range(8):
                query = qo[i // 4, :, pl.ds(i % 4 * HD, HD)].astype(F32)
                m, l, o = add_entry(0, i, query, key, value)
                if i < 4:
                    out_ref[0, :, pl.ds(i * HD, HD)] = (o / l).astype(BF16)
                else:
                    mo[i], lo[i], oo[i] = m, l, o
            for copy in b_z:
                copy.wait_recv()
    from_sibling(LONG, wrap_y(y + step_l * LONG))

    fresh_bias = bias_row[...].astype(F32)
    for j in range(NZ - 1):
        fresh_bias = fresh_bias + bias_z[j].astype(F32)
    e_send.append(entry(1, acc[...], fresh_bias[:1]))

    for copy in die + [q_send, b_die] + b_y + b_z + p_send + z_send + zg + e_send[:1]:
        copy.wait_send()
    for group_of in (hz, hx, long_send, short_send, al, ash, df):
        for copy in group_of.values():
            copy.wait_send()

    e_send[1].wait_recv()
    key, value = new_pair(1)
    for i in range(4, 8):
        query = qo[1, :, pl.ds((i - 4) * HD, HD)].astype(F32)
        m, l, o = add_entry(1, i, query, key, value)
        out_ref[1, :, pl.ds((i - 4) * HD, HD)] = (o / l).astype(BF16)
    e_send[1].wait_send()


def on_device(hidden, queries, kv_cache, lengths, weights, kv_bias, owner_group):
    sem = pltpu.SemaphoreType.DMA
    vmem = pltpu.VMEM
    any_spec = pl.BlockSpec(memory_space=pl.ANY)
    vmem_spec = pl.BlockSpec(memory_space=pltpu.VMEM)
    scratch = [
        vmem((D, HD), BF16), vmem((HALF, HD), BF16),
        vmem((LONG, CHUNK, HD), BF16), vmem((SHORT, CHUNK, HD), BF16),
        vmem((NZ - 1, QUART, HD), BF16), vmem((D, HD), BF16),
        vmem((2, 8, ROWS, 1024), BF16), vmem((ROWS * 64, 256), BF16),
        vmem((2, ROWS, 512), BF16), vmem((2, ROWS, 512), BF16),
        vmem((8, ROWS, HD), F32), vmem((8, ROWS, HD), F32), vmem((8, ROWS, HD), F32),
        vmem((8, ROWS, HD), BF16), vmem((ROWS, HD), F32),
        vmem((8, ROWS, HD), BF16), vmem((ROWS, HD), F32),
        vmem((ROWS, HD), F32), vmem((2, ROWS, HD), F32), vmem((2, ROWS, HD), F32),
        vmem((16, HD), BF16), vmem((16, HD), BF16), vmem((16, HD), BF16),
        vmem((NY - 1, 16, HD), BF16), vmem((16, HD), BF16), vmem((NZ - 1, 16, HD), BF16),
        vmem((2, ROWS, HD), BF16), vmem((2, ROWS, HD), BF16), vmem((ROWS, HD), F32),
        sem((4,)), sem((NY,)), sem((NY,)),
        sem((LONG, 4)), sem((LONG, 4)), sem((SHORT, 4)), sem((SHORT, 4)),
        sem((3,)), sem((3,)), sem((3,)), sem((3,)),
        sem((LONG, 4)), sem((LONG, 4)), sem((SHORT, 4)), sem((SHORT, 4)),
        sem((NY, 4)), sem((NY, 4)),
        sem((2,)), sem((2,)), sem((2, 2, 3)), sem((2, 2, 3)),
        sem, sem, sem((2,)), sem((2,)), sem((2,)), sem((2,)),
        sem, sem, sem((NY - 1,)), sem((NY - 1,)), sem((NZ - 1,)), sem((NZ - 1,)),
    ]
    return pl.pallas_call(
        kernel,
        out_shape=jax.ShapeDtypeStruct((2, ROWS, 512), BF16),
        in_specs=[any_spec] * 4 + [vmem_spec] * 2 + [pl.BlockSpec(memory_space=pltpu.SMEM)],
        out_specs=vmem_spec,
        scratch_shapes=scratch,
        compiler_params=pltpu.CompilerParams(
            collective_id=0, has_side_effects=True, vmem_limit_bytes=56 << 20),
    )(
        weights.reshape(D, HD), kv_cache.reshape(ROWS * 64, 256), hidden,
        queries.reshape(2, ROWS, 512), lengths.reshape(1, ROWS), kv_bias, owner_group,
    )


def solution(mesh):
    in_specs = (
        P(None, "group", "tp"),
        P(None, "group", "tp", None),
        P("group", "tp", None, None),
        P("group"),
        P("group", None, "tp"),
        P("group", "tp"),
        P(),
    )
    out_specs = P(None, "group", "tp")
    return jax.shard_map(
        on_device, mesh=mesh, in_specs=in_specs, out_specs=out_specs, check_vma=False
    )
```

```python
import math

import jax
import jax.numpy as jnp
from jax import lax
from jax.experimental import pallas as pl
from jax.experimental.pallas import tpu as pltpu
from jax.sharding import PartitionSpec as P

MESH = pl.DeviceIdType.MESH
BF16 = jnp.bfloat16
F32 = jnp.float32
NEG = -1e30
NY, NZ, NX = 8, 4, 4
LONG, SHORT = 4, 3
ROWS, HD, STRIP = 64, 128, 1024
SCALE2 = math.log2(math.e) / math.sqrt(128.0)


def remote(src, dst, send_sem, recv_sem, device):
    return pltpu.make_async_remote_copy(
        src_ref=src, dst_ref=dst, send_sem=send_sem, recv_sem=recv_sem,
        device_id=device, device_id_type=MESH,
    )


def dot_t(a, b):
    return lax.dot_general(a, b, (((1,), (1,)), ((), ())), preferred_element_type=F32)


def kernel(
    w_hbm, kv_hbm, hid_hbm, q_hbm, len_ref, bias_ref, owner_ref, out_ref,
    wv, xbuf, rl, rs, zr, wf, feat, hb, hf, kvv, qo, qp,
    oo, mo, lo, po, pml, ro, rml, lenc, cosf, sinf,
    bias_mine, bias_die, bias_chip, bias_y, bias_row, bias_z,
    part_sib, part_own, part_in, ring_out, ring_in, kvown, kvpeer,
    loc_sem, die_r, rl_r, rs_r, z_r, zg_r, one_s, one_r,
):
    group = lax.axis_index("group")
    tp = lax.axis_index("tp")
    core = group % 2
    y = (group // 2) % NY
    zh = group // (2 * NY)
    x = tp % NX
    zl = tp // NX
    step_l = 1 - 2 * core
    other_core = 1 - core
    lead = core == zl

    def at(zz, yy, cc):
        return (zz * (2 * NY) + yy * 2 + cc, tp)

    def wrap_y(v):
        return (v + 4 * NY) % NY

    sibling = at(zh, y, other_core)
    ahead = at(zh, wrap_y(y + step_l), core)
    behind = at(zh, wrap_y(y - step_l), core)
    z_peers = [at((zh + j) % NZ, y, core) for j in range(1, NZ)]
    y_peers = [at(zh, (y + j) % NY, core) for j in range(1, NY)]
    partner_tp = (tp + NX) % (2 * NX)
    partner = (group, partner_tp)
    x_peers = [(group, zl * NX + (x + j) % NX) for j in range(1, NX)]

    kinds = (
        "die", "long", "short", "z", "zg", "feat_die", "feat_y", "feat_z", "feat_x",
        "hz", "hx", "q", "po", "pml", "bd", "by", "bz", "part", "ring", "e0", "e1",
    )
    slot = {name: i for i, name in enumerate(kinds)}

    def push(kind, src, dst, device, recv_sem=None):
        recv_sem = one_r.at[slot[kind]] if recv_sem is None else recv_sem
        copy = remote(src, dst, one_s.at[slot[kind]], recv_sem, device)
        copy.start()
        return copy

    def take(kind, ref):
        remote(ref, ref, one_s.at[slot[kind]], one_r.at[slot[kind]], sibling).wait_recv()

    def sent(kind, ref):
        remote(ref, ref, one_s.at[slot[kind]], one_r.at[slot[kind]], sibling).wait_send()

    w_copy = pltpu.make_async_copy(w_hbm, wv, loc_sem.at[1])
    q_copy = pltpu.make_async_copy(q_hbm, qo, loc_sem.at[3])
    h_copy = pltpu.make_async_copy(hid_hbm.at[0], hf.at[tp], loc_sem.at[2])
    kv_copy = pltpu.make_async_copy(kv_hbm, kvv, loc_sem.at[0])
    w_copy.start()
    q_copy.start()
    h_copy.start()
    kv_copy.start()

    @pl.when(lead)
    def _():
        pltpu.make_async_copy(hid_hbm.at[1], hb.at[core], loc_sem.at[4]).start()

    barrier = pltpu.get_barrier_semaphore()
    everyone = [sibling, partner] + x_peers + z_peers + y_peers
    for other in everyone:
        pl.semaphore_signal(barrier, inc=1, device_id=other, device_id_type=MESH)
    pl.semaphore_wait(barrier, len(everyone))

    order = []
    for s in range(LONG):
        order.append(wrap_y(y + step_l * (LONG - s)))
        if s < SHORT:
            order.append(wrap_y(y - step_l * (SHORT - s)))
    order.append(y)

    for n in range(NY):
        if n == NY - 1:
            chunk = y
        elif n % 2 == 0:
            chunk = wrap_y(y - step_l * (LONG - n // 2))
        else:
            chunk = wrap_y(y + step_l * (SHORT - n // 2))
        push("die", w_hbm.at[pl.ds(4 * other_core, 4), chunk], xbuf.at[:, chunk], sibling,
             die_r.at[n])

    @pl.when(jnp.logical_not(lead))
    def _():
        push("feat_die", hid_hbm.at[1], hb.at[core], sibling)

    push("q", q_hbm, qp, partner)
    push("hz", hid_hbm.at[0], hf.at[tp], partner)
    for j in range(NX - 1):
        push("hx", hid_hbm.at[0], hf.at[tp], x_peers[j])

    owner = owner_ref[0]
    mine_w = jnp.full((1, HD), (owner == group).astype(F32)).astype(BF16)
    sib_w = jnp.full((1, HD), (owner == group + 1 - 2 * core).astype(F32)).astype(BF16)

    bias_mine[...] = jnp.broadcast_to(bias_ref[...] * mine_w, (16, HD))
    push("bd", bias_mine, bias_die, sibling)

    w_copy.wait()

    def combine(n):
        chunk = order[n]
        remote(xbuf.at[:, chunk], xbuf.at[:, chunk], one_s.at[0], die_r.at[n], sibling).wait_recv()
        for i in range(4):
            xbuf[i, chunk] = wv[4 * core + i, chunk] * mine_w + xbuf[i, chunk] * sib_w

    quarters = [(zh + 1 + n) % NZ for n in range(4)]
    long_send, short_send = {}, {}

    def reduce_step(s):
        chunk = wrap_y(y + step_l * (LONG - s))
        other = wrap_y(y - step_l * (SHORT - s))
        for n in range(4):
            if s == 0:
                src = xbuf.at[quarters[n], chunk]
            else:
                long_send[s - 1, n].wait_recv()
                rl[s - 1, n] = rl[s - 1, n] + xbuf[quarters[n], chunk]
                src = rl.at[s - 1, n]
            long_send[s, n] = push("long", src, rl.at[s, n], ahead, rl_r.at[s, n])
            if s < SHORT:
                if s == 0:
                    src = xbuf.at[quarters[n], other]
                else:
                    short_send[s - 1, n].wait_recv()
                    rs[s - 1, n] = rs[s - 1, n] + xbuf[quarters[n], other]
                    src = rs.at[s - 1, n]
                short_send[s, n] = push("short", src, rs.at[s, n], behind, rs_r.at[s, n])

    combine(0)
    combine(1)
    reduce_step(0)
    for n in range(2, NY):
        combine(n)

    @pl.when(lead)
    def _():
        pltpu.make_async_copy(hid_hbm.at[1], hb.at[core], loc_sem.at[4]).wait()
        take("feat_die", hb.at[other_core])
        pltpu.make_async_copy(
            hb.at[:, :, pl.ds(pl.multiple_of(y * HD, HD), HD)], feat.at[x, y], loc_sem.at[4]
        ).start()
        for j in range(1, NY):
            yy = (y + j) % NY
            push("feat_y", hb.at[:, :, pl.ds(pl.multiple_of(yy * HD, HD), HD)], feat.at[x, y],
                 y_peers[j - 1])

    lens = jnp.broadcast_to(len_ref[...].astype(F32), (ROWS, ROWS))
    diag = lax.broadcasted_iota(jnp.int32, (ROWS, ROWS), 0) == lax.broadcasted_iota(
        jnp.int32, (ROWS, ROWS), 1)
    len_col = jnp.sum(jnp.where(diag, lens, 0.0), axis=1, keepdims=True)
    lenc[...] = jnp.broadcast_to(len_col, (ROWS, HD))

    def attend(block):
        kept = []
        for sub in range(2):
            r0 = block * 16 + sub * 8
            pieces = []
            for src in (qo, qp):
                for s in range(2):
                    for j in range(4):
                        part = src[s, pl.ds(block * 16, 16), pl.ds(j * HD, HD)].astype(F32)
                        pieces.append(part[sub * 8:sub * 8 + 8])
            lhs = jnp.concatenate(pieces, axis=0).astype(BF16)
            cache = pl.ds(r0 * 64, 512)
            scores = dot_t(lhs, kvv[cache, pl.ds(0, HD)]).reshape(16, 8, 512)
            row_id = lax.broadcasted_iota(jnp.int32, (8, 512), 0)
            col_id = lax.broadcasted_iota(jnp.int32, (8, 512), 1)
            length = lenc[pl.ds(r0, 8), :][:, :1]
            pos = (col_id % 64 + zl * 64).astype(F32)
            usable = jnp.logical_and(col_id // 64 == row_id, pos < length)[None]
            peak = jnp.max(jnp.where(usable, scores, NEG), axis=2, keepdims=True)
            weight = jnp.exp2(jnp.where(usable, (scores - peak) * SCALE2, NEG))
            total = jnp.sum(weight, axis=2, keepdims=True)
            weighted = jnp.dot(
                weight.astype(BF16).reshape(128, 512), kvv[cache, pl.ds(HD, HD)],
                preferred_element_type=F32).reshape(16, 8, HD)
            rows = pl.ds(r0, 8)
            oo[:, rows] = weighted[:8]
            mo[:, rows] = jnp.broadcast_to(peak[:8], (8, 8, HD))
            lo[:, rows] = jnp.broadcast_to(total[:8], (8, 8, HD))
            kept.append(weighted[8:])
            lane = lax.broadcasted_iota(jnp.int32, (8, HD), 1)
            packed = jnp.zeros((8, HD), F32)
            for i in range(8):
                packed = jnp.where(lane == i, peak[8 + i], packed)
                packed = jnp.where(lane == 8 + i, total[8 + i], packed)
            pml[rows] = packed
        po[:, pl.ds(block * 16, 16)] = jnp.concatenate(kept, axis=1).astype(BF16)

    q_copy.wait()
    kv_copy.wait()
    take("bd", bias_die)
    bias_chip[...] = bias_mine[...] + bias_die[...]
    for j in range(NY - 1):
        push("by", bias_chip, bias_y.at[j], y_peers[j])
    take("q", qp)
    attend(0)

    reduce_step(1)

    take("hz", hf.at[0])
    for j in range(NX - 1):
        push("hx", hf.at[partner_tp], hf.at[partner_tp], x_peers[j])
    attend(1)

    reduce_step(2)

    def spread_feat():
        for j in range(NX - 1):
            push("feat_x", feat.at[x], feat.at[x], x_peers[j])

    attend(2)

    @pl.when(lead)
    def _():
        pltpu.make_async_copy(
            hb.at[:, :, pl.ds(pl.multiple_of(y * HD, HD), HD)], feat.at[x, y], loc_sem.at[4]
        ).wait()
        take("feat_y", feat.at[0, pl.ds(0, NY - 1)])
        push("feat_z", feat.at[x], feat.at[x], partner)
        spread_feat()

    reduce_step(3)
    attend(3)
    push("po", po, ro, partner)
    push("pml", pml, rml, partner)

    take("by", bias_y)
    total_bias = bias_chip[...]
    for j in range(NY - 1):
        total_bias = total_bias + bias_y[j]
    bias_row[...] = total_bias
    for j in range(NZ - 1):
        push("bz", bias_row, bias_z.at[j], z_peers[j])

    z_send = []
    for n in range(4):
        short_send[SHORT - 1, n].wait_recv()
        long_send[LONG - 1, n].wait_recv()
        rl[LONG - 1, n] = rl[LONG - 1, n] + rs[SHORT - 1, n] + xbuf[quarters[n], y]
        if n < 3:
            z_send.append(push("z", rl.at[LONG - 1, n], zr.at[n], z_peers[n], z_r.at[n]))

    @pl.when(jnp.logical_not(lead))
    def _():
        take("feat_z", feat.at[0])
        spread_feat()

    lane = lax.broadcasted_iota(jnp.int32, (ROWS, HD), 1)
    freq = jnp.exp(-((lane % 64).astype(F32) * (2.0 / HD)) * math.log(1000000.0))
    is_key = tp < NX
    for s in range(2):
        angle = (lenc[...] + float(s)) * freq
        sine = jnp.sin(angle)
        cosf[s] = jnp.where(is_key, jnp.cos(angle), 1.0)
        sinf[s] = jnp.where(is_key, jnp.where(lane < 64, -sine, sine), 0.0)

    total_w = rl[LONG - 1, 3]
    for j in range(NZ - 1):
        z_send[j].wait_recv()
        total_w = total_w + zr[j]
    wf[zh] = total_w
    zg = [push("zg", wf.at[zh], wf.at[zh], z_peers[j], zg_r.at[j]) for j in range(NZ - 1)]

    def entry(s, total, bias):
        total = total + bias
        turned = total * cosf[s] + pltpu.roll(total, 64, 1) * sinf[s]
        kvown[s] = turned.astype(BF16)
        push(f"e{s}", kvown.at[s], kvpeer.at[s], partner)

    h_copy.wait()
    take("hx", hf.at[pl.ds(0, 2 * (NX - 1))])
    total = jnp.zeros((ROWS, HD), F32)
    for t in range(8):
        total = total + jnp.dot(
            hf[t], wv[t].reshape(STRIP, HD), preferred_element_type=F32)
    entry(0, total, bias_ref[...].astype(F32))

    def product(i, cc):
        rows = feat[i, :, cc].reshape(NY * ROWS, HD)
        return jnp.dot(rows, wf[i], preferred_element_type=F32)

    take("feat_x", feat.at[pl.ds(0, NX - 1)])
    part_sib[...] = product(zh, other_core)
    part_own[...] = product(zh, core)
    for j in range(NZ - 1):
        i = (zh - j - 1 + NZ) % NZ
        zg[j].wait_recv()
        part_sib[...] += product(i, other_core)
        if j == NZ - 2:
            push("part", part_sib, part_in, sibling)
        part_own[...] += product(i, core)
    take("part", part_in)
    part_own[...] += part_in[...]
    ring_out[...] = part_own[...].astype(BF16).reshape(NY, ROWS, HD)
    for j in range(1, NY):
        push("ring", ring_out.at[(y + j) % NY], ring_in.at[j - 1], y_peers[j - 1])

    def add_entry(s, i, query, key, value):
        score = jnp.sum(query * key, axis=1, keepdims=True)
        old = mo[i]
        peak = jnp.maximum(old, score)
        keep = jnp.exp2((old - peak) * SCALE2)
        weight = jnp.exp2((score - peak) * SCALE2)
        return (
            peak,
            lo[i] * keep + weight,
            oo[i] * keep + weight.astype(BF16).astype(F32) * value,
        )

    def new_pair(s):
        own, other = kvown[s].astype(F32), kvpeer[s].astype(F32)
        return jnp.where(is_key, own, other), jnp.where(is_key, other, own)

    take("po", ro)
    take("pml", rml)
    take("e0", kvpeer.at[0])
    key, value = new_pair(0)
    for i in range(8):
        m2 = rml[:, i:i + 1]
        l2 = rml[:, 8 + i:9 + i]
        m1 = mo[i]
        peak = jnp.maximum(m1, m2)
        e1 = jnp.exp2((m1 - peak) * SCALE2)
        e2 = jnp.exp2((m2 - peak) * SCALE2)
        mo[i] = peak
        lo[i] = lo[i] * e1 + l2 * e2
        oo[i] = oo[i] * e1 + ro[i].astype(F32) * e2
        query = qo[i // 4, :, pl.ds(i % 4 * HD, HD)].astype(F32)
        m, l, o = add_entry(0, i, query, key, value)
        if i < 4:
            out_ref[0, :, pl.ds(i * HD, HD)] = (o / l).astype(BF16)
        else:
            mo[i], lo[i], oo[i] = m, l, o
    take("bz", bias_z)
    fresh_bias = bias_row[...].astype(F32)
    for j in range(NZ - 1):
        fresh_bias = fresh_bias + bias_z[j].astype(F32)

    sent("die", xbuf)
    sent("long", rl)
    sent("short", rs)
    sent("z", zr)
    sent("zg", zr)
    sent("hz", hf.at[0])
    sent("hx", hf.at[pl.ds(0, 2 * (NX - 1))])
    sent("feat_x", feat.at[pl.ds(0, NX - 1)])
    sent("q", qp)
    sent("po", po)
    sent("pml", pml)
    sent("bd", bias_die)
    sent("by", bias_y)
    sent("bz", bias_z)
    sent("part", part_sib)
    sent("e0", kvown.at[0])

    @pl.when(lead)
    def _():
        sent("feat_y", feat.at[0, pl.ds(0, NY - 1)])
        sent("feat_z", feat.at[0])

    @pl.when(jnp.logical_not(lead))
    def _():
        sent("feat_die", hb.at[0])

    own_rows = pl.ds(pl.multiple_of(y * ROWS, ROWS), ROWS)
    total = part_own[own_rows]
    take("ring", ring_in)
    for j in range(NY - 1):
        total = total + ring_in[j].astype(F32)
    entry(1, total, fresh_bias[:1])
    sent("ring", ring_in)

    take("e1", kvpeer.at[1])
    key, value = new_pair(1)
    for i in range(4, 8):
        query = qo[1, :, pl.ds((i - 4) * HD, HD)].astype(F32)
        m, l, o = add_entry(1, i, query, key, value)
        out_ref[1, :, pl.ds((i - 4) * HD, HD)] = (o / l).astype(BF16)
    sent("e1", kvown.at[1])


def on_device(hidden, queries, kv_cache, lengths, weights, kv_bias, owner_group):
    sem = pltpu.SemaphoreType.DMA
    vmem = pltpu.VMEM
    any_spec = pl.BlockSpec(memory_space=pl.ANY)
    vmem_spec = pl.BlockSpec(memory_space=pltpu.VMEM)
    wide = (8, ROWS, HD)
    scratch = [
        vmem((8, NY, HD, HD), BF16), vmem((4, NY, HD, HD), BF16),
        vmem((LONG, 4, HD, HD), BF16), vmem((SHORT, 4, HD, HD), BF16),
        vmem((NZ - 1, HD, HD), BF16), vmem((4, HD, HD), BF16),
        vmem((NX, NY, 2, ROWS, HD), BF16), vmem((2, ROWS, STRIP), BF16),
        vmem((8, ROWS, STRIP), BF16), vmem((ROWS * 64, 256), BF16),
        vmem((2, ROWS, 512), BF16), vmem((2, ROWS, 512), BF16),
        vmem(wide, F32), vmem(wide, F32), vmem(wide, F32),
        vmem(wide, BF16), vmem((ROWS, HD), F32),
        vmem(wide, BF16), vmem((ROWS, HD), F32),
        vmem((ROWS, HD), F32), vmem((2, ROWS, HD), F32), vmem((2, ROWS, HD), F32),
        vmem((16, HD), BF16), vmem((16, HD), BF16), vmem((16, HD), BF16),
        vmem((NY - 1, 16, HD), BF16), vmem((16, HD), BF16), vmem((NZ - 1, 16, HD), BF16),
        vmem((NY * ROWS, HD), F32), vmem((NY * ROWS, HD), F32), vmem((NY * ROWS, HD), F32),
        vmem(wide, BF16), vmem((NY - 1, ROWS, HD), BF16),
        vmem((2, ROWS, HD), BF16), vmem((2, ROWS, HD), BF16),
        sem((5,)), sem((NY,)), sem((LONG, 4)), sem((SHORT, 4)),
        sem((3,)), sem((3,)), sem((21,)), sem((21,)),
    ]
    return pl.pallas_call(
        kernel,
        out_shape=jax.ShapeDtypeStruct((2, ROWS, 512), BF16),
        in_specs=[any_spec] * 4 + [vmem_spec] * 2 + [pl.BlockSpec(memory_space=pltpu.SMEM)],
        out_specs=vmem_spec,
        scratch_shapes=scratch,
        compiler_params=pltpu.CompilerParams(
            collective_id=0, has_side_effects=True, vmem_limit_bytes=56 << 20),
    )(
        weights.reshape(8, NY, HD, HD), kv_cache.reshape(ROWS * 64, 256), hidden,
        queries.reshape(2, ROWS, 512), lengths.reshape(1, ROWS), kv_bias, owner_group,
    )


def solution(mesh):
    in_specs = (
        P(None, "group", "tp"),
        P(None, "group", "tp", None),
        P("group", "tp", None, None),
        P("group"),
        P("group", None, "tp"),
        P("group", "tp"),
        P(),
    )
    out_specs = P(None, "group", "tp")
    return jax.shard_map(
        on_device, mesh=mesh, in_specs=in_specs, out_specs=out_specs, check_vma=False
    )
```

```python
import math

import jax
import jax.numpy as jnp
from jax import lax
from jax.experimental import pallas as pl
from jax.experimental.pallas import tpu as pltpu
from jax.sharding import PartitionSpec as P

MESH = pl.DeviceIdType.MESH
BF16 = jnp.bfloat16
F32 = jnp.float32
NEG = -1e30
NY, NZ, NX = 8, 4, 4
LONG, SHORT = 4, 3
ROWS, HD, STRIP = 64, 128, 1024
SCALE2 = math.log2(math.e) / math.sqrt(128.0)


def remote(src, dst, send_sem, recv_sem, device):
    return pltpu.make_async_remote_copy(
        src_ref=src, dst_ref=dst, send_sem=send_sem, recv_sem=recv_sem,
        device_id=device, device_id_type=MESH,
    )


def dot_t(a, b):
    return lax.dot_general(a, b, (((1,), (1,)), ((), ())), preferred_element_type=F32)


def kernel(
    w_hbm, kv_hbm, hid_hbm, q_hbm, len_hbm, bias_hbm, owner_hbm, out_ref,
    len_ref, bias_ref, owner_ref,
    wv, xbuf, rl, rs, zr, wf, feat, hf, kvv, qo, qp,
    oo, mo, lo, po, pml, ro, rml, lenc, cosf, sinf,
    bias_mine, bias_die, bias_chip, bias_y, bias_row, bias_z,
    part_sib, part_own, part_in, ring_out, ring_in, kvown, kvpeer,
    loc_sem, die_r, rl_r, rs_r, z_r, zg_r, one_s, one_r,
):
    group = lax.axis_index("group")
    tp = lax.axis_index("tp")
    core = group % 2
    y = (group // 2) % NY
    zh = group // (2 * NY)
    x = tp % NX
    zl = tp // NX
    step_l = 1 - 2 * core
    other_core = 1 - core
    lead = core == zl

    def at(zz, yy, cc):
        return (zz * (2 * NY) + yy * 2 + cc, tp)

    def wrap_y(v):
        return (v + 4 * NY) % NY

    sibling = at(zh, y, other_core)
    ahead = at(zh, wrap_y(y + step_l), core)
    behind = at(zh, wrap_y(y - step_l), core)
    z_peers = [at((zh + j) % NZ, y, core) for j in range(1, NZ)]
    y_peers = [at(zh, (y + j) % NY, core) for j in range(1, NY)]
    partner_tp = (tp + NX) % (2 * NX)
    partner = (group, partner_tp)
    x_peers = [(group, zl * NX + (x + j) % NX) for j in range(1, NX)]

    kinds = (
        "die", "long", "short", "z", "zg", "feat_die", "feat_y", "feat_z", "feat_x",
        "hz", "hx", "q", "po", "pml", "bd", "by", "bz", "part", "ring", "e0", "e1",
    )
    slot = {name: i for i, name in enumerate(kinds)}

    def push(kind, src, dst, device, recv_sem=None):
        recv_sem = one_r.at[slot[kind]] if recv_sem is None else recv_sem
        copy = remote(src, dst, one_s.at[slot[kind]], recv_sem, device)
        copy.start()
        return copy

    def take(kind, ref):
        remote(ref, ref, one_s.at[slot[kind]], one_r.at[slot[kind]], sibling).wait_recv()

    def sent(kind, ref):
        remote(ref, ref, one_s.at[slot[kind]], one_r.at[slot[kind]], sibling).wait_send()

    w_copy = pltpu.make_async_copy(w_hbm, wv, loc_sem.at[1])
    q_copy = pltpu.make_async_copy(q_hbm, qo, loc_sem.at[3])
    h_copy = pltpu.make_async_copy(hid_hbm.at[0], hf.at[tp], loc_sem.at[2])
    kv_copy = pltpu.make_async_copy(kv_hbm, kvv, loc_sem.at[0])
    w_copy.start()
    q_copy.start()
    h_copy.start()
    kv_copy.start()

    small = [
        pltpu.make_async_copy(len_hbm, len_ref, loc_sem.at[5]),
        pltpu.make_async_copy(bias_hbm, bias_ref, loc_sem.at[6]),
        pltpu.make_async_copy(owner_hbm, owner_ref, loc_sem.at[7]),
    ]
    for copy in small:
        copy.start()

    def strip(yy):
        return hid_hbm.at[1, :, pl.ds(pl.multiple_of(yy * HD, HD), HD)]

    @pl.when(lead)
    def _():
        pltpu.make_async_copy(strip(y), feat.at[x, y, core], loc_sem.at[4]).start()

    barrier = pltpu.get_barrier_semaphore()
    cross = [at(zh, (y + j) % NY, other_core) for j in range(1, NY)]
    everyone = [sibling, partner] + x_peers + z_peers + y_peers + cross
    for other in everyone:
        pl.semaphore_signal(barrier, inc=1, device_id=other, device_id_type=MESH)
    pl.semaphore_wait(barrier, len(everyone))

    order = []
    for s in range(LONG):
        order.append(wrap_y(y + step_l * (LONG - s)))
        if s < SHORT:
            order.append(wrap_y(y - step_l * (SHORT - s)))
    order.append(y)

    for n in range(NY):
        if n == NY - 1:
            chunk = y
        elif n % 2 == 0:
            chunk = wrap_y(y - step_l * (LONG - n // 2))
        else:
            chunk = wrap_y(y + step_l * (SHORT - n // 2))
        push("die", w_hbm.at[pl.ds(4 * other_core, 4), chunk], xbuf.at[:, chunk], sibling,
             die_r.at[n])
        if n == 1:
            for j in range(1, NY):
                yy = (y + j) % NY
                push("feat_y", strip(yy), feat.at[x, y, core], at(zh, yy, zl))

    @pl.when(jnp.logical_not(lead))
    def _():
        push("feat_die", strip(y), feat.at[x, y, core], sibling)

    push("q", q_hbm, qp, partner)
    push("hz", hid_hbm.at[0], hf.at[tp], partner)
    for j in range(NX - 1):
        push("hx", hid_hbm.at[0], hf.at[tp], x_peers[j])

    for copy in small:
        copy.wait()
    owner = owner_ref[0]
    mine_w = jnp.full((1, HD), (owner == group).astype(F32)).astype(BF16)
    sib_w = jnp.full((1, HD), (owner == group + 1 - 2 * core).astype(F32)).astype(BF16)

    bias_mine[...] = jnp.broadcast_to(bias_ref[...] * mine_w, (16, HD))
    push("bd", bias_mine, bias_die, sibling)

    w_copy.wait()

    def combine(n):
        chunk = order[n]
        remote(xbuf.at[:, chunk], xbuf.at[:, chunk], one_s.at[0], die_r.at[n], sibling).wait_recv()
        for i in range(4):
            xbuf[i, chunk] = wv[4 * core + i, chunk] * mine_w + xbuf[i, chunk] * sib_w

    quarters = [(zh + 1 + n) % NZ for n in range(4)]
    long_send, short_send = {}, {}

    def reduce_step(s):
        chunk = wrap_y(y + step_l * (LONG - s))
        other = wrap_y(y - step_l * (SHORT - s))
        for n in range(4):
            if s == 0:
                src = xbuf.at[quarters[n], chunk]
            else:
                long_send[s - 1, n].wait_recv()
                rl[s - 1, n] = rl[s - 1, n] + xbuf[quarters[n], chunk]
                src = rl.at[s - 1, n]
            long_send[s, n] = push("long", src, rl.at[s, n], ahead, rl_r.at[s, n])
            if s < SHORT:
                if s == 0:
                    src = xbuf.at[quarters[n], other]
                else:
                    short_send[s - 1, n].wait_recv()
                    rs[s - 1, n] = rs[s - 1, n] + xbuf[quarters[n], other]
                    src = rs.at[s - 1, n]
                short_send[s, n] = push("short", src, rs.at[s, n], behind, rs_r.at[s, n])

    combine(0)
    combine(1)
    reduce_step(0)
    for n in range(2, NY):
        combine(n)

    lens = jnp.broadcast_to(len_ref[...].astype(F32), (ROWS, ROWS))
    diag = lax.broadcasted_iota(jnp.int32, (ROWS, ROWS), 0) == lax.broadcasted_iota(
        jnp.int32, (ROWS, ROWS), 1)
    len_col = jnp.sum(jnp.where(diag, lens, 0.0), axis=1, keepdims=True)
    lenc[...] = jnp.broadcast_to(len_col, (ROWS, HD))

    def attend(block):
        kept = []
        for sub in range(2):
            r0 = block * 16 + sub * 8
            pieces = []
            for src in (qo, qp):
                for s in range(2):
                    for j in range(4):
                        part = src[s, pl.ds(block * 16, 16), pl.ds(j * HD, HD)].astype(F32)
                        pieces.append(part[sub * 8:sub * 8 + 8])
            lhs = jnp.concatenate(pieces, axis=0).astype(BF16)
            cache = pl.ds(r0 * 64, 512)
            scores = dot_t(lhs, kvv[cache, pl.ds(0, HD)]).reshape(16, 8, 512)
            row_id = lax.broadcasted_iota(jnp.int32, (8, 512), 0)
            col_id = lax.broadcasted_iota(jnp.int32, (8, 512), 1)
            length = lenc[pl.ds(r0, 8), :][:, :1]
            pos = (col_id % 64 + zl * 64).astype(F32)
            usable = jnp.logical_and(col_id // 64 == row_id, pos < length)[None]
            peak = jnp.max(jnp.where(usable, scores, NEG), axis=2, keepdims=True)
            weight = jnp.exp2(jnp.where(usable, (scores - peak) * SCALE2, NEG))
            total = jnp.sum(weight, axis=2, keepdims=True)
            weighted = jnp.dot(
                weight.astype(BF16).reshape(128, 512), kvv[cache, pl.ds(HD, HD)],
                preferred_element_type=F32).reshape(16, 8, HD)
            rows = pl.ds(r0, 8)
            oo[:, rows] = weighted[:8]
            mo[:, rows] = jnp.broadcast_to(peak[:8], (8, 8, HD))
            lo[:, rows] = jnp.broadcast_to(total[:8], (8, 8, HD))
            kept.append(weighted[8:])
            lane = lax.broadcasted_iota(jnp.int32, (8, HD), 1)
            packed = jnp.zeros((8, HD), F32)
            for i in range(8):
                packed = jnp.where(lane == i, peak[8 + i], packed)
                packed = jnp.where(lane == 8 + i, total[8 + i], packed)
            pml[rows] = packed
        po[:, pl.ds(block * 16, 16)] = jnp.concatenate(kept, axis=1).astype(BF16)

    q_copy.wait()
    kv_copy.wait()
    take("bd", bias_die)
    bias_chip[...] = bias_mine[...] + bias_die[...]
    for j in range(NY - 1):
        push("by", bias_chip, bias_y.at[j], y_peers[j])
    take("q", qp)
    attend(0)

    reduce_step(1)

    def spread_feat():
        for j in range(NX - 1):
            push("feat_x", feat.at[x], feat.at[x], x_peers[j])

    @pl.when(lead)
    def _():
        pltpu.make_async_copy(strip(y), feat.at[x, y, core], loc_sem.at[4]).wait()
        take("feat_y", feat.at[0, pl.ds(0, NY - 1)])
        take("feat_die", feat.at[0, 0, 0])
        push("feat_z", feat.at[x], feat.at[x], partner)
        spread_feat()

    take("hz", hf.at[0])
    for j in range(NX - 1):
        push("hx", hf.at[partner_tp], hf.at[partner_tp], x_peers[j])
    attend(1)

    reduce_step(2)
    attend(2)

    reduce_step(3)

    @pl.when(jnp.logical_not(lead))
    def _():
        take("feat_z", feat.at[0])
        spread_feat()

    attend(3)
    push("po", po, ro, partner)
    push("pml", pml, rml, partner)

    take("by", bias_y)
    total_bias = bias_chip[...]
    for j in range(NY - 1):
        total_bias = total_bias + bias_y[j]
    bias_row[...] = total_bias
    for j in range(NZ - 1):
        push("bz", bias_row, bias_z.at[j], z_peers[j])

    z_send = []
    for n in range(4):
        short_send[SHORT - 1, n].wait_recv()
        long_send[LONG - 1, n].wait_recv()
        rl[LONG - 1, n] = rl[LONG - 1, n] + rs[SHORT - 1, n] + xbuf[quarters[n], y]
        if n < 3:
            z_send.append(push("z", rl.at[LONG - 1, n], zr.at[n], z_peers[n], z_r.at[n]))

    lane = lax.broadcasted_iota(jnp.int32, (ROWS, HD), 1)
    freq = jnp.exp(-((lane % 64).astype(F32) * (2.0 / HD)) * math.log(1000000.0))
    is_key = tp < NX
    for s in range(2):
        angle = (lenc[...] + float(s)) * freq
        sine = jnp.sin(angle)
        cosf[s] = jnp.where(is_key, jnp.cos(angle), 1.0)
        sinf[s] = jnp.where(is_key, jnp.where(lane < 64, -sine, sine), 0.0)

    total_w = rl[LONG - 1, 3]
    for j in range(NZ - 1):
        z_send[j].wait_recv()
        total_w = total_w + zr[j]
    wf[zh] = total_w
    zg = [push("zg", wf.at[zh], wf.at[zh], z_peers[j], zg_r.at[j]) for j in range(NZ - 1)]

    def entry(s, total, bias):
        total = total + bias
        turned = total * cosf[s] + pltpu.roll(total, 64, 1) * sinf[s]
        kvown[s] = turned.astype(BF16)
        push(f"e{s}", kvown.at[s], kvpeer.at[s], partner)

    h_copy.wait()
    take("hx", hf.at[pl.ds(0, 2 * (NX - 1))])
    total = jnp.zeros((ROWS, HD), F32)
    for t in range(8):
        total = total + jnp.dot(
            hf[t], wv[t].reshape(STRIP, HD), preferred_element_type=F32)
    entry(0, total, bias_ref[...].astype(F32))

    def product(i, cc):
        rows = feat[i, :, cc].reshape(NY * ROWS, HD)
        return jnp.dot(rows, wf[i], preferred_element_type=F32)

    take("feat_x", feat.at[pl.ds(0, NX - 1)])
    part_sib[...] = product(zh, other_core)
    part_own[...] = product(zh, core)
    for j in range(NZ - 1):
        i = (zh - j - 1 + NZ) % NZ
        zg[j].wait_recv()
        part_sib[...] += product(i, other_core)
        if j == NZ - 2:
            push("part", part_sib, part_in, sibling)
        part_own[...] += product(i, core)
    take("part", part_in)
    part_own[...] += part_in[...]
    ring_out[...] = part_own[...].astype(BF16).reshape(NY, ROWS, HD)
    for j in range(1, NY):
        push("ring", ring_out.at[(y + j) % NY], ring_in.at[j - 1], y_peers[j - 1])

    def add_entry(s, i, query, key, value):
        score = jnp.sum(query * key, axis=1, keepdims=True)
        old = mo[i]
        peak = jnp.maximum(old, score)
        keep = jnp.exp2((old - peak) * SCALE2)
        weight = jnp.exp2((score - peak) * SCALE2)
        return (
            peak,
            lo[i] * keep + weight,
            oo[i] * keep + weight.astype(BF16).astype(F32) * value,
        )

    def new_pair(s):
        own, other = kvown[s].astype(F32), kvpeer[s].astype(F32)
        return jnp.where(is_key, own, other), jnp.where(is_key, other, own)

    take("po", ro)
    take("pml", rml)
    take("e0", kvpeer.at[0])
    key, value = new_pair(0)
    for i in range(8):
        m2 = rml[:, i:i + 1]
        l2 = rml[:, 8 + i:9 + i]
        m1 = mo[i]
        peak = jnp.maximum(m1, m2)
        e1 = jnp.exp2((m1 - peak) * SCALE2)
        e2 = jnp.exp2((m2 - peak) * SCALE2)
        mo[i] = peak
        lo[i] = lo[i] * e1 + l2 * e2
        oo[i] = oo[i] * e1 + ro[i].astype(F32) * e2
        query = qo[i // 4, :, pl.ds(i % 4 * HD, HD)].astype(F32)
        m, l, o = add_entry(0, i, query, key, value)
        if i < 4:
            out_ref[0, :, pl.ds(i * HD, HD)] = (o / l).astype(BF16)
        else:
            mo[i], lo[i], oo[i] = m, l, o
    take("bz", bias_z)
    fresh_bias = bias_row[...].astype(F32)
    for j in range(NZ - 1):
        fresh_bias = fresh_bias + bias_z[j].astype(F32)

    sent("die", xbuf)
    sent("long", rl)
    sent("short", rs)
    sent("z", zr)
    sent("zg", zr)
    sent("hz", hf.at[0])
    sent("hx", hf.at[pl.ds(0, 2 * (NX - 1))])
    sent("feat_x", feat.at[pl.ds(0, NX - 1)])
    sent("q", qp)
    sent("po", po)
    sent("pml", pml)
    sent("bd", bias_die)
    sent("by", bias_y)
    sent("bz", bias_z)
    sent("part", part_sib)
    sent("e0", kvown.at[0])
    sent("feat_y", ring_in)

    @pl.when(lead)
    def _():
        sent("feat_z", feat.at[0])

    @pl.when(jnp.logical_not(lead))
    def _():
        sent("feat_die", kvown.at[0])

    own_rows = pl.ds(pl.multiple_of(y * ROWS, ROWS), ROWS)
    total = part_own[own_rows]
    take("ring", ring_in)
    for j in range(NY - 1):
        total = total + ring_in[j].astype(F32)
    entry(1, total, fresh_bias[:1])
    sent("ring", ring_in)

    take("e1", kvpeer.at[1])
    key, value = new_pair(1)
    for i in range(4, 8):
        query = qo[1, :, pl.ds((i - 4) * HD, HD)].astype(F32)
        m, l, o = add_entry(1, i, query, key, value)
        out_ref[1, :, pl.ds((i - 4) * HD, HD)] = (o / l).astype(BF16)
    sent("e1", kvown.at[1])


def on_device(hidden, queries, kv_cache, lengths, weights, kv_bias, owner_group):
    sem = pltpu.SemaphoreType.DMA
    vmem = pltpu.VMEM
    any_spec = pl.BlockSpec(memory_space=pl.ANY)
    vmem_spec = pl.BlockSpec(memory_space=pltpu.VMEM)
    wide = (8, ROWS, HD)
    scratch = [
        vmem((1, ROWS), jnp.int32), vmem((1, HD), BF16), pltpu.SMEM((1,), jnp.int32),
        vmem((8, NY, HD, HD), BF16), vmem((4, NY, HD, HD), BF16),
        vmem((LONG, 4, HD, HD), BF16), vmem((SHORT, 4, HD, HD), BF16),
        vmem((NZ - 1, HD, HD), BF16), vmem((4, HD, HD), BF16),
        vmem((NX, NY, 2, ROWS, HD), BF16),
        vmem((8, ROWS, STRIP), BF16), vmem((ROWS * 64, 256), BF16),
        vmem((2, ROWS, 512), BF16), vmem((2, ROWS, 512), BF16),
        vmem(wide, F32), vmem(wide, F32), vmem(wide, F32),
        vmem(wide, BF16), vmem((ROWS, HD), F32),
        vmem(wide, BF16), vmem((ROWS, HD), F32),
        vmem((ROWS, HD), F32), vmem((2, ROWS, HD), F32), vmem((2, ROWS, HD), F32),
        vmem((16, HD), BF16), vmem((16, HD), BF16), vmem((16, HD), BF16),
        vmem((NY - 1, 16, HD), BF16), vmem((16, HD), BF16), vmem((NZ - 1, 16, HD), BF16),
        vmem((NY * ROWS, HD), F32), vmem((NY * ROWS, HD), F32), vmem((NY * ROWS, HD), F32),
        vmem(wide, BF16), vmem((NY - 1, ROWS, HD), BF16),
        vmem((2, ROWS, HD), BF16), vmem((2, ROWS, HD), BF16),
        sem((8,)), sem((NY,)), sem((LONG, 4)), sem((SHORT, 4)),
        sem((3,)), sem((3,)), sem((21,)), sem((21,)),
    ]
    return pl.pallas_call(
        kernel,
        out_shape=jax.ShapeDtypeStruct((2, ROWS, 512), BF16),
        in_specs=[any_spec] * 7,
        out_specs=vmem_spec,
        scratch_shapes=scratch,
        compiler_params=pltpu.CompilerParams(
            collective_id=0, has_side_effects=True, vmem_limit_bytes=56 << 20),
    )(
        weights.reshape(8, NY, HD, HD), kv_cache.reshape(ROWS * 64, 256), hidden,
        queries.reshape(2, ROWS, 512), lengths.reshape(1, ROWS), kv_bias,
        owner_group,
    )


def solution(mesh):
    in_specs = (
        P(None, "group", "tp"),
        P(None, "group", "tp", None),
        P("group", "tp", None, None),
        P("group"),
        P("group", None, "tp"),
        P("group", "tp"),
        P(),
    )
    out_specs = P(None, "group", "tp")
    return jax.shard_map(
        on_device, mesh=mesh, in_specs=in_specs, out_specs=out_specs, check_vma=False
    )
```

```python
import math

import jax
import jax.numpy as jnp
from jax import lax
from jax.experimental import pallas as pl
from jax.experimental.pallas import tpu as pltpu
from jax.sharding import PartitionSpec as P

MESH = pl.DeviceIdType.MESH
BF16 = jnp.bfloat16
F32 = jnp.float32
NEG = -1e30
NY, NZ, NX = 8, 4, 4
LONG, SHORT = 4, 3
ROWS, HD, STRIP = 64, 128, 1024
SCALE2 = math.log2(math.e) / math.sqrt(128.0)


def remote(src, dst, send_sem, recv_sem, device):
    return pltpu.make_async_remote_copy(
        src_ref=src, dst_ref=dst, send_sem=send_sem, recv_sem=recv_sem,
        device_id=device, device_id_type=MESH,
    )


def dot_t(a, b):
    return lax.dot_general(a, b, (((1,), (1,)), ((), ())), preferred_element_type=F32)


def kernel(
    w_hbm, kv_hbm, hid_hbm, q_hbm, len_hbm, bias_hbm, owner_hbm, out_ref,
    len_ref, bias_ref, owner_ref,
    wv, xbuf, rl, rs, zr, wf, feat, hf, kvv, qo, qp,
    oo, mo, lo, po, pml, ro, rml, lenc, cosf, sinf,
    bias_mine, bias_die, bias_chip, bias_y, bias_row, bias_z,
    part_sib, part_own, part_in, ring_out, ring_in, kvown, kvpeer,
    loc_sem, die_r, rl_r, rs_r, z_r, zg_r, one_s, one_r,
):
    group = lax.axis_index("group")
    tp = lax.axis_index("tp")
    core = group % 2
    y = (group // 2) % NY
    zh = group // (2 * NY)
    x = tp % NX
    zl = tp // NX
    step_l = 1 - 2 * core
    other_core = 1 - core
    lead = core == zl

    def at(zz, yy, cc):
        return (zz * (2 * NY) + yy * 2 + cc, tp)

    def wrap_y(v):
        return (v + 4 * NY) % NY

    sibling = at(zh, y, other_core)
    ahead = at(zh, wrap_y(y + step_l), core)
    behind = at(zh, wrap_y(y - step_l), core)
    z_peers = [at((zh + j) % NZ, y, core) for j in range(1, NZ)]
    y_peers = [at(zh, (y + j) % NY, core) for j in range(1, NY)]
    partner_tp = (tp + NX) % (2 * NX)
    partner = (group, partner_tp)
    x_peers = [(group, zl * NX + (x + j) % NX) for j in range(1, NX)]

    kinds = (
        "die", "long", "short", "z", "zg", "feat_die", "feat_y", "feat_z", "feat_x",
        "hz", "hx", "q", "po", "pml", "bd", "by", "bz", "part", "ring", "e0", "e1",
    )
    slot = {name: i for i, name in enumerate(kinds)}

    def push(kind, src, dst, device, recv_sem=None):
        recv_sem = one_r.at[slot[kind]] if recv_sem is None else recv_sem
        copy = remote(src, dst, one_s.at[slot[kind]], recv_sem, device)
        copy.start()
        return copy

    def take(kind, ref):
        remote(ref, ref, one_s.at[slot[kind]], one_r.at[slot[kind]], sibling).wait_recv()

    def sent(kind, ref):
        remote(ref, ref, one_s.at[slot[kind]], one_r.at[slot[kind]], sibling).wait_send()

    w_copy = pltpu.make_async_copy(w_hbm, wv, loc_sem.at[1])
    q_copy = pltpu.make_async_copy(q_hbm, qo, loc_sem.at[3])
    h_copy = pltpu.make_async_copy(hid_hbm.at[0], hf.at[tp], loc_sem.at[2])
    kv_copy = pltpu.make_async_copy(kv_hbm, kvv, loc_sem.at[0])
    w_copy.start()
    q_copy.start()
    h_copy.start()
    kv_copy.start()

    small = [
        pltpu.make_async_copy(len_hbm, len_ref, loc_sem.at[5]),
        pltpu.make_async_copy(bias_hbm, bias_ref, loc_sem.at[6]),
        pltpu.make_async_copy(owner_hbm, owner_ref, loc_sem.at[7]),
    ]
    for copy in small:
        copy.start()

    def strip(yy):
        return hid_hbm.at[1, :, pl.ds(pl.multiple_of(yy * HD, HD), HD)]

    @pl.when(lead)
    def _():
        pltpu.make_async_copy(strip(y), feat.at[x, y, core], loc_sem.at[4]).start()

    barrier = pltpu.get_barrier_semaphore()
    cross = [at(zh, (y + j) % NY, other_core) for j in range(1, NY)]
    everyone = [sibling, partner] + x_peers + z_peers + y_peers + cross
    for other in everyone:
        pl.semaphore_signal(barrier, inc=1, device_id=other, device_id_type=MESH)
    pl.semaphore_wait(barrier, len(everyone))

    order = []
    for s in range(LONG):
        order.append(wrap_y(y + step_l * (LONG - s)))
        if s < SHORT:
            order.append(wrap_y(y - step_l * (SHORT - s)))
    order.append(y)

    for n in range(NY):
        if n == NY - 1:
            chunk = y
        elif n % 2 == 0:
            chunk = wrap_y(y - step_l * (LONG - n // 2))
        else:
            chunk = wrap_y(y + step_l * (SHORT - n // 2))
        push("die", w_hbm.at[pl.ds(4 * other_core, 4), chunk], xbuf.at[:, chunk], sibling,
             die_r.at[n])
        if n == 1:
            for j in range(1, NY):
                yy = (y + j) % NY
                push("feat_y", strip(yy), feat.at[x, y, core], at(zh, yy, zl))

    @pl.when(jnp.logical_not(lead))
    def _():
        push("feat_die", strip(y), feat.at[x, y, core], sibling)

    push("q", q_hbm, qp, partner)
    push("hz", hid_hbm.at[0], hf.at[tp], partner)
    for j in range(NX - 1):
        push("hx", hid_hbm.at[0], hf.at[tp], x_peers[j])

    for copy in small:
        copy.wait()
    owner = owner_ref[0]
    mine_w = jnp.full((1, HD), (owner == group).astype(F32)).astype(BF16)
    sib_w = jnp.full((1, HD), (owner == group + 1 - 2 * core).astype(F32)).astype(BF16)

    bias_mine[...] = jnp.broadcast_to(bias_ref[...] * mine_w, (16, HD))
    push("bd", bias_mine, bias_die, sibling)

    w_copy.wait()

    def combine(n):
        chunk = order[n]
        remote(xbuf.at[:, chunk], xbuf.at[:, chunk], one_s.at[0], die_r.at[n], sibling).wait_recv()
        for i in range(4):
            xbuf[i, chunk] = wv[4 * core + i, chunk] * mine_w + xbuf[i, chunk] * sib_w

    quarters = [(zh + 1 + n) % NZ for n in range(4)]
    long_send, short_send = {}, {}

    def reduce_step(s):
        chunk = wrap_y(y + step_l * (LONG - s))
        other = wrap_y(y - step_l * (SHORT - s))
        for n in range(4):
            if s == 0:
                src = xbuf.at[quarters[n], chunk]
            else:
                long_send[s - 1, n].wait_recv()
                rl[s - 1, n] = rl[s - 1, n] + xbuf[quarters[n], chunk]
                src = rl.at[s - 1, n]
            long_send[s, n] = push("long", src, rl.at[s, n], ahead, rl_r.at[s, n])
            if s < SHORT:
                if s == 0:
                    src = xbuf.at[quarters[n], other]
                else:
                    short_send[s - 1, n].wait_recv()
                    rs[s - 1, n] = rs[s - 1, n] + xbuf[quarters[n], other]
                    src = rs.at[s - 1, n]
                short_send[s, n] = push("short", src, rs.at[s, n], behind, rs_r.at[s, n])

    combine(0)
    combine(1)
    reduce_step(0)
    for n in range(2, NY):
        combine(n)

    lens = jnp.broadcast_to(len_ref[...].astype(F32), (ROWS, ROWS))
    diag = lax.broadcasted_iota(jnp.int32, (ROWS, ROWS), 0) == lax.broadcasted_iota(
        jnp.int32, (ROWS, ROWS), 1)
    len_col = jnp.sum(jnp.where(diag, lens, 0.0), axis=1, keepdims=True)
    lenc[...] = jnp.broadcast_to(len_col, (ROWS, HD))

    def attend(block):
        kept = []
        for sub in range(2):
            r0 = block * 16 + sub * 8
            pieces = []
            for src in (qo, qp):
                for s in range(2):
                    for j in range(4):
                        part = src[s, pl.ds(block * 16, 16), pl.ds(j * HD, HD)].astype(F32)
                        pieces.append(part[sub * 8:sub * 8 + 8])
            lhs = jnp.concatenate(pieces, axis=0).astype(BF16)
            cache = pl.ds(r0 * 64, 512)
            scores = dot_t(lhs, kvv[cache, pl.ds(0, HD)]).reshape(16, 8, 512)
            row_id = lax.broadcasted_iota(jnp.int32, (8, 512), 0)
            col_id = lax.broadcasted_iota(jnp.int32, (8, 512), 1)
            length = lenc[pl.ds(r0, 8), :][:, :1]
            pos = (col_id % 64 + zl * 64).astype(F32)
            usable = jnp.logical_and(col_id // 64 == row_id, pos < length)[None]
            peak = jnp.max(jnp.where(usable, scores, NEG), axis=2, keepdims=True)
            weight = jnp.exp2(jnp.where(usable, (scores - peak) * SCALE2, NEG))
            total = jnp.sum(weight, axis=2, keepdims=True)
            weighted = jnp.dot(
                weight.astype(BF16).reshape(128, 512), kvv[cache, pl.ds(HD, HD)],
                preferred_element_type=F32).reshape(16, 8, HD)
            rows = pl.ds(r0, 8)
            oo[:, rows] = weighted[:8]
            mo[:, rows] = jnp.broadcast_to(peak[:8], (8, 8, HD))
            lo[:, rows] = jnp.broadcast_to(total[:8], (8, 8, HD))
            kept.append(weighted[8:])
            lane = lax.broadcasted_iota(jnp.int32, (8, HD), 1)
            packed = jnp.zeros((8, HD), F32)
            for i in range(8):
                packed = jnp.where(lane == i, peak[8 + i], packed)
                packed = jnp.where(lane == 8 + i, total[8 + i], packed)
            pml[rows] = packed
        po[:, pl.ds(block * 16, 16)] = jnp.concatenate(kept, axis=1).astype(BF16)

    q_copy.wait()
    kv_copy.wait()
    take("bd", bias_die)
    bias_chip[...] = bias_mine[...] + bias_die[...]
    for j in range(NY - 1):
        push("by", bias_chip, bias_y.at[j], y_peers[j])
    take("q", qp)
    attend(0)

    reduce_step(1)

    def spread_feat():
        for j in range(NX - 1):
            push("feat_x", feat.at[x], feat.at[x], x_peers[j])

    @pl.when(lead)
    def _():
        pltpu.make_async_copy(strip(y), feat.at[x, y, core], loc_sem.at[4]).wait()
        take("feat_y", feat.at[0, pl.ds(0, NY - 1)])
        take("feat_die", feat.at[0, 0, 0])
        push("feat_z", feat.at[x], feat.at[x], partner)
        spread_feat()

    take("hz", hf.at[0])
    for j in range(NX - 1):
        push("hx", hf.at[partner_tp], hf.at[partner_tp], x_peers[j])
    attend(1)

    reduce_step(2)
    attend(2)

    reduce_step(3)

    @pl.when(jnp.logical_not(lead))
    def _():
        take("feat_z", feat.at[0])
        spread_feat()

    attend(3)
    push("po", po, ro, partner)
    push("pml", pml, rml, partner)

    take("by", bias_y)
    total_bias = bias_chip[...]
    for j in range(NY - 1):
        total_bias = total_bias + bias_y[j]
    bias_row[...] = total_bias
    for j in range(NZ - 1):
        push("bz", bias_row, bias_z.at[j], z_peers[j])

    z_send = []
    for n in range(4):
        short_send[SHORT - 1, n].wait_recv()
        long_send[LONG - 1, n].wait_recv()
        rl[LONG - 1, n] = rl[LONG - 1, n] + rs[SHORT - 1, n] + xbuf[quarters[n], y]
        if n < 3:
            z_send.append(push("z", rl.at[LONG - 1, n], zr.at[n], z_peers[n], z_r.at[n]))

    lane = lax.broadcasted_iota(jnp.int32, (ROWS, HD), 1)
    freq = jnp.exp(-((lane % 64).astype(F32) * (2.0 / HD)) * math.log(1000000.0))
    is_key = tp < NX
    for s in range(2):
        angle = (lenc[...] + float(s)) * freq
        sine = jnp.sin(angle)
        cosf[s] = jnp.where(is_key, jnp.cos(angle), 1.0)
        sinf[s] = jnp.where(is_key, jnp.where(lane < 64, -sine, sine), 0.0)

    total_w = rl[LONG - 1, 3]
    for j in range(NZ - 1):
        z_send[j].wait_recv()
        total_w = total_w + zr[j]
    wf[zh] = total_w
    zg = [push("zg", wf.at[zh], wf.at[zh], z_peers[j], zg_r.at[j]) for j in range(NZ - 1)]

    def entry(s, total, bias):
        total = total + bias
        turned = total * cosf[s] + pltpu.roll(total, 64, 1) * sinf[s]
        kvown[s] = turned.astype(BF16)
        push(f"e{s}", kvown.at[s], kvpeer.at[s], partner)

    h_copy.wait()
    take("hx", hf.at[pl.ds(0, 2 * (NX - 1))])
    total = jnp.zeros((ROWS, HD), F32)
    for t in range(8):
        total = total + jnp.dot(
            hf[t], wv[t].reshape(STRIP, HD), preferred_element_type=F32)
    entry(0, total, bias_ref[...].astype(F32))

    def product(i, cc):
        rows = feat[i, :, cc].reshape(NY * ROWS, HD)
        return jnp.dot(rows, wf[i], preferred_element_type=F32)

    take("feat_x", feat.at[pl.ds(0, NX - 1)])
    part_sib[...] = product(zh, other_core)
    part_own[...] = product(zh, core)
    for j in range(NZ - 1):
        i = (zh - j - 1 + NZ) % NZ
        zg[j].wait_recv()
        part_sib[...] += product(i, other_core)
        if j == NZ - 2:
            push("part", part_sib, part_in, sibling)
        part_own[...] += product(i, core)
    take("part", part_in)
    part_own[...] += part_in[...]
    ring_out[...] = part_own[...].astype(BF16).reshape(NY, ROWS, HD)
    for j in range(1, NY):
        push("ring", ring_out.at[(y + j) % NY], ring_in.at[j - 1], y_peers[j - 1])

    def add_entry(s, i, query, key, value):
        score = jnp.sum(query * key, axis=1, keepdims=True)
        old = mo[i]
        peak = jnp.maximum(old, score)
        keep = jnp.exp2((old - peak) * SCALE2)
        weight = jnp.exp2((score - peak) * SCALE2)
        return (
            peak,
            lo[i] * keep + weight,
            oo[i] * keep + weight.astype(BF16).astype(F32) * value,
        )

    def new_pair(s):
        own, other = kvown[s].astype(F32), kvpeer[s].astype(F32)
        return jnp.where(is_key, own, other), jnp.where(is_key, other, own)

    take("po", ro)
    take("pml", rml)
    take("e0", kvpeer.at[0])
    key, value = new_pair(0)
    for i in range(8):
        m2 = rml[:, i:i + 1]
        l2 = rml[:, 8 + i:9 + i]
        m1 = mo[i]
        peak = jnp.maximum(m1, m2)
        e1 = jnp.exp2((m1 - peak) * SCALE2)
        e2 = jnp.exp2((m2 - peak) * SCALE2)
        mo[i] = peak
        lo[i] = lo[i] * e1 + l2 * e2
        oo[i] = oo[i] * e1 + ro[i].astype(F32) * e2
        query = qo[i // 4, :, pl.ds(i % 4 * HD, HD)].astype(F32)
        m, l, o = add_entry(0, i, query, key, value)
        if i < 4:
            out_ref[0, :, pl.ds(i * HD, HD)] = (o / l).astype(BF16)
        else:
            mo[i], lo[i], oo[i] = m, l, o
    take("bz", bias_z)
    fresh_bias = bias_row[...].astype(F32)
    for j in range(NZ - 1):
        fresh_bias = fresh_bias + bias_z[j].astype(F32)

    sent("die", xbuf)
    sent("long", rl)
    sent("short", rs)
    sent("z", zr)
    sent("zg", zr)
    sent("hz", hf.at[0])
    sent("hx", hf.at[pl.ds(0, 2 * (NX - 1))])
    sent("feat_x", feat.at[pl.ds(0, NX - 1)])
    sent("q", qp)
    sent("po", po)
    sent("pml", pml)
    sent("bd", bias_die)
    sent("by", bias_y)
    sent("bz", bias_z)
    sent("part", part_sib)
    sent("e0", kvown.at[0])
    sent("feat_y", ring_in)

    @pl.when(lead)
    def _():
        sent("feat_z", feat.at[0])

    @pl.when(jnp.logical_not(lead))
    def _():
        sent("feat_die", kvown.at[0])

    own_rows = pl.ds(pl.multiple_of(y * ROWS, ROWS), ROWS)
    total = part_own[own_rows]
    take("ring", ring_in)
    for j in range(NY - 1):
        total = total + ring_in[j].astype(F32)
    entry(1, total, fresh_bias[:1])
    sent("ring", ring_in)

    take("e1", kvpeer.at[1])
    key, value = new_pair(1)
    for i in range(4, 8):
        query = qo[1, :, pl.ds((i - 4) * HD, HD)].astype(F32)
        m, l, o = add_entry(1, i, query, key, value)
        out_ref[1, :, pl.ds((i - 4) * HD, HD)] = (o / l).astype(BF16)
    sent("e1", kvown.at[1])


def on_device(hidden, queries, kv_cache, lengths, weights, kv_bias, owner_group):
    sem = pltpu.SemaphoreType.DMA
    vmem = pltpu.VMEM
    any_spec = pl.BlockSpec(memory_space=pl.ANY)
    vmem_spec = pl.BlockSpec(memory_space=pltpu.VMEM)
    wide = (8, ROWS, HD)
    scratch = [
        vmem((1, ROWS), jnp.int32), vmem((1, HD), BF16), pltpu.SMEM((1,), jnp.int32),
        vmem((8, NY, HD, HD), BF16), vmem((4, NY, HD, HD), BF16),
        vmem((LONG, 4, HD, HD), BF16), vmem((SHORT, 4, HD, HD), BF16),
        vmem((NZ - 1, HD, HD), BF16), vmem((4, HD, HD), BF16),
        vmem((NX, NY, 2, ROWS, HD), BF16),
        vmem((8, ROWS, STRIP), BF16), vmem((ROWS * 64, 256), BF16),
        vmem((2, ROWS, 512), BF16), vmem((2, ROWS, 512), BF16),
        vmem(wide, F32), vmem(wide, F32), vmem(wide, F32),
        vmem(wide, BF16), vmem((ROWS, HD), F32),
        vmem(wide, BF16), vmem((ROWS, HD), F32),
        vmem((ROWS, HD), F32), vmem((2, ROWS, HD), F32), vmem((2, ROWS, HD), F32),
        vmem((16, HD), BF16), vmem((16, HD), BF16), vmem((16, HD), BF16),
        vmem((NY - 1, 16, HD), BF16), vmem((16, HD), BF16), vmem((NZ - 1, 16, HD), BF16),
        vmem((NY * ROWS, HD), F32), vmem((NY * ROWS, HD), F32), vmem((NY * ROWS, HD), F32),
        vmem(wide, BF16), vmem((NY - 1, ROWS, HD), BF16),
        vmem((2, ROWS, HD), BF16), vmem((2, ROWS, HD), BF16),
        sem((8,)), sem((NY,)), sem((LONG, 4)), sem((SHORT, 4)),
        sem((3,)), sem((3,)), sem((21,)), sem((21,)),
    ]
    return pl.pallas_call(
        kernel,
        out_shape=pltpu.VMEM((2, ROWS, 512), BF16),
        in_specs=[any_spec] * 7,
        out_specs=vmem_spec,
        scratch_shapes=scratch,
        compiler_params=pltpu.CompilerParams(
            collective_id=0, has_side_effects=True, vmem_limit_bytes=56 << 20),
    )(
        weights.reshape(8, NY, HD, HD), kv_cache.reshape(ROWS * 64, 256), hidden,
        queries.reshape(2, ROWS, 512), lengths.reshape(1, ROWS), kv_bias,
        owner_group,
    )


def solution(mesh):
    in_specs = (
        P(None, "group", "tp"),
        P(None, "group", "tp", None),
        P("group", "tp", None, None),
        P("group"),
        P("group", None, "tp"),
        P("group", "tp"),
        P(),
    )
    out_specs = P(None, "group", "tp")
    return jax.shard_map(
        on_device, mesh=mesh, in_specs=in_specs, out_specs=out_specs, check_vma=False
    )
```

```python
import math

import jax
import jax.numpy as jnp
from jax import lax
from jax.experimental import pallas as pl
from jax.experimental.pallas import tpu as pltpu
from jax.sharding import PartitionSpec as P

MESH = pl.DeviceIdType.MESH
BF16 = jnp.bfloat16
F32 = jnp.float32
NEG = -1e30
NY, NZ, NX = 8, 4, 4
LONG, SHORT = 4, 3
ROWS, HD, STRIP = 64, 128, 1024
SCALE2 = math.log2(math.e) / math.sqrt(128.0)


def remote(src, dst, send_sem, recv_sem, device):
    return pltpu.make_async_remote_copy(
        src_ref=src, dst_ref=dst, send_sem=send_sem, recv_sem=recv_sem,
        device_id=device, device_id_type=MESH,
    )


def dot_t(a, b):
    return lax.dot_general(a, b, (((1,), (1,)), ((), ())), preferred_element_type=F32)


def kernel(
    w_hbm, kv_hbm, hid_hbm, q_hbm, len_hbm, bias_hbm, owner_hbm, out_ref,
    len_ref, bias_ref, owner_ref,
    wv, xbuf, rl, rs, zr, wf, feat, hf, kvv, qo, qp,
    oo, mo, lo, po, pml, ro, rml, lenc, cosf, sinf,
    bias_mine, bias_die, bias_chip, bias_y, bias_row, bias_z,
    part_sib, part_own, part_in, ring_out, ring_in, kvown, kvpeer,
    loc_sem, die_r, rl_r, rs_r, z_r, zg_r, one_s, one_r,
):
    group = lax.axis_index("group")
    tp = lax.axis_index("tp")
    core = group % 2
    y = (group // 2) % NY
    zh = group // (2 * NY)
    x = tp % NX
    zl = tp // NX
    step_l = 1 - 2 * core
    other_core = 1 - core
    lead = core == zl

    def at(zz, yy, cc):
        return (zz * (2 * NY) + yy * 2 + cc, tp)

    def wrap_y(v):
        return (v + 4 * NY) % NY

    sibling = at(zh, y, other_core)
    ahead = at(zh, wrap_y(y + step_l), core)
    behind = at(zh, wrap_y(y - step_l), core)
    z_peers = [at((zh + j) % NZ, y, core) for j in range(1, NZ)]
    y_peers = [at(zh, (y + j) % NY, core) for j in range(1, NY)]
    partner_tp = (tp + NX) % (2 * NX)
    partner = (group, partner_tp)
    x_peers = [(group, zl * NX + (x + j) % NX) for j in range(1, NX)]

    kinds = (
        "die", "long", "short", "z", "zg", "feat_die", "feat_y", "feat_z", "feat_x",
        "hz", "hx", "q", "po", "pml", "bd", "by", "bz", "part", "ring", "e0", "e1",
    )
    slot = {name: i for i, name in enumerate(kinds)}

    def push(kind, src, dst, device, recv_sem=None):
        recv_sem = one_r.at[slot[kind]] if recv_sem is None else recv_sem
        copy = remote(src, dst, one_s.at[slot[kind]], recv_sem, device)
        copy.start()
        return copy

    def take(kind, ref):
        remote(ref, ref, one_s.at[slot[kind]], one_r.at[slot[kind]], sibling).wait_recv()

    def sent(kind, ref):
        remote(ref, ref, one_s.at[slot[kind]], one_r.at[slot[kind]], sibling).wait_send()

    w_copy = pltpu.make_async_copy(w_hbm, wv, loc_sem.at[1])
    q_copy = pltpu.make_async_copy(q_hbm, qo, loc_sem.at[3])
    h_copy = pltpu.make_async_copy(hid_hbm.at[0], hf.at[tp], loc_sem.at[2])
    kv_copy = pltpu.make_async_copy(kv_hbm, kvv, loc_sem.at[0])
    w_copy.start()
    q_copy.start()
    h_copy.start()
    kv_copy.start()

    small = [
        pltpu.make_async_copy(len_hbm, len_ref, loc_sem.at[5]),
        pltpu.make_async_copy(bias_hbm, bias_ref, loc_sem.at[6]),
        pltpu.make_async_copy(owner_hbm, owner_ref, loc_sem.at[7]),
    ]
    for copy in small:
        copy.start()

    def strip(yy):
        return hid_hbm.at[1, :, pl.ds(pl.multiple_of(yy * HD, HD), HD)]

    @pl.when(lead)
    def _():
        pltpu.make_async_copy(strip(y), feat.at[x, y, core], loc_sem.at[4]).start()

    barrier = pltpu.get_barrier_semaphore()
    cross = [at(zh, (y + j) % NY, other_core) for j in range(1, NY)]
    everyone = [sibling, partner] + x_peers + z_peers + y_peers + cross
    for other in everyone:
        pl.semaphore_signal(barrier, inc=1, device_id=other, device_id_type=MESH)
    pl.semaphore_wait(barrier, len(everyone))

    order = []
    for s in range(LONG):
        order.append(wrap_y(y + step_l * (LONG - s)))
        if s < SHORT:
            order.append(wrap_y(y - step_l * (SHORT - s)))
    order.append(y)

    for n in range(NY):
        if n == NY - 1:
            chunk = y
        elif n % 2 == 0:
            chunk = wrap_y(y - step_l * (LONG - n // 2))
        else:
            chunk = wrap_y(y + step_l * (SHORT - n // 2))
        push("die", w_hbm.at[pl.ds(4 * other_core, 4), chunk], xbuf.at[:, chunk], sibling,
             die_r.at[n])
        if n == 1:
            for j in range(1, NY):
                yy = (y + j) % NY
                push("feat_y", strip(yy), feat.at[x, y, core], at(zh, yy, zl))

    @pl.when(jnp.logical_not(lead))
    def _():
        push("feat_die", strip(y), feat.at[x, y, core], sibling)

    push("q", q_hbm, qp, partner)
    push("hz", hid_hbm.at[0], hf.at[tp], partner)
    for j in range(NX - 1):
        push("hx", hid_hbm.at[0], hf.at[tp], x_peers[j])

    for copy in small:
        copy.wait()
    owner = owner_ref[0]
    mine_w = jnp.full((1, HD), (owner == group).astype(F32)).astype(BF16)
    sib_w = jnp.full((1, HD), (owner == group + 1 - 2 * core).astype(F32)).astype(BF16)

    bias_mine[...] = jnp.broadcast_to(bias_ref[...] * mine_w, (16, HD))
    push("bd", bias_mine, bias_die, sibling)

    w_copy.wait()

    def combine(n):
        chunk = order[n]
        remote(xbuf.at[:, chunk], xbuf.at[:, chunk], one_s.at[0], die_r.at[n], sibling).wait_recv()
        for i in range(4):
            xbuf[i, chunk] = wv[4 * core + i, chunk] * mine_w + xbuf[i, chunk] * sib_w

    quarters = [(zh + 1 + n) % NZ for n in range(4)]
    long_send, short_send = {}, {}

    def reduce_step(s):
        chunk = wrap_y(y + step_l * (LONG - s))
        other = wrap_y(y - step_l * (SHORT - s))
        for n in range(4):
            if s == 0:
                src = xbuf.at[quarters[n], chunk]
            else:
                long_send[s - 1, n].wait_recv()
                rl[s - 1, n] = rl[s - 1, n] + xbuf[quarters[n], chunk]
                src = rl.at[s - 1, n]
            long_send[s, n] = push("long", src, rl.at[s, n], ahead, rl_r.at[s, n])
            if s < SHORT:
                if s == 0:
                    src = xbuf.at[quarters[n], other]
                else:
                    short_send[s - 1, n].wait_recv()
                    rs[s - 1, n] = rs[s - 1, n] + xbuf[quarters[n], other]
                    src = rs.at[s - 1, n]
                short_send[s, n] = push("short", src, rs.at[s, n], behind, rs_r.at[s, n])

    combine(0)
    combine(1)
    reduce_step(0)
    for n in range(2, NY):
        combine(n)

    lens = jnp.broadcast_to(len_ref[...].astype(F32), (ROWS, ROWS))
    diag = lax.broadcasted_iota(jnp.int32, (ROWS, ROWS), 0) == lax.broadcasted_iota(
        jnp.int32, (ROWS, ROWS), 1)
    len_col = jnp.sum(jnp.where(diag, lens, 0.0), axis=1, keepdims=True)
    lenc[...] = jnp.broadcast_to(len_col, (ROWS, HD))

    def attend(block):
        kept = []
        for sub in range(2):
            r0 = block * 16 + sub * 8
            pieces = []
            for src in (qo, qp):
                for s in range(2):
                    for j in range(4):
                        part = src[s, pl.ds(block * 16, 16), pl.ds(j * HD, HD)].astype(F32)
                        pieces.append(part[sub * 8:sub * 8 + 8])
            lhs = jnp.concatenate(pieces, axis=0).astype(BF16)
            cache = pl.ds(r0 * 64, 512)
            scores = dot_t(lhs, kvv[cache, pl.ds(0, HD)]).reshape(16, 8, 512)
            row_id = lax.broadcasted_iota(jnp.int32, (8, 512), 0)
            col_id = lax.broadcasted_iota(jnp.int32, (8, 512), 1)
            length = lenc[pl.ds(r0, 8), :][:, :1]
            pos = (col_id % 64 + zl * 64).astype(F32)
            usable = jnp.logical_and(col_id // 64 == row_id, pos < length)[None]
            peak = jnp.max(jnp.where(usable, scores, NEG), axis=2, keepdims=True)
            weight = jnp.exp2(jnp.where(usable, (scores - peak) * SCALE2, NEG))
            total = jnp.sum(weight, axis=2, keepdims=True)
            weighted = jnp.dot(
                weight.astype(BF16).reshape(128, 512), kvv[cache, pl.ds(HD, HD)],
                preferred_element_type=F32).reshape(16, 8, HD)
            rows = pl.ds(r0, 8)
            oo[:, rows] = weighted[:8]
            mo[:, rows] = jnp.broadcast_to(peak[:8], (8, 8, HD))
            lo[:, rows] = jnp.broadcast_to(total[:8], (8, 8, HD))
            kept.append(weighted[8:])
            lane = lax.broadcasted_iota(jnp.int32, (8, HD), 1)
            packed = jnp.zeros((8, HD), F32)
            for i in range(8):
                packed = jnp.where(lane == i, peak[8 + i], packed)
                packed = jnp.where(lane == 8 + i, total[8 + i], packed)
            pml[rows] = packed
        po[:, pl.ds(block * 16, 16)] = jnp.concatenate(kept, axis=1).astype(BF16)

    q_copy.wait()
    kv_copy.wait()
    take("bd", bias_die)
    bias_chip[...] = bias_mine[...] + bias_die[...]
    take("q", qp)
    attend(0)

    reduce_step(1)

    def spread_feat():
        for j in range(NX - 1):
            push("feat_x", feat.at[x], feat.at[x], x_peers[j])

    @pl.when(lead)
    def _():
        pltpu.make_async_copy(strip(y), feat.at[x, y, core], loc_sem.at[4]).wait()
        take("feat_y", feat.at[0, pl.ds(0, NY - 1)])
        take("feat_die", feat.at[0, 0, 0])
        push("feat_z", feat.at[x], feat.at[x], partner)
        spread_feat()

    take("hz", hf.at[0])
    for j in range(NX - 1):
        push("hx", hf.at[partner_tp], hf.at[partner_tp], x_peers[j])
    attend(1)

    reduce_step(2)
    attend(2)

    reduce_step(3)

    @pl.when(jnp.logical_not(lead))
    def _():
        take("feat_z", feat.at[0])
        spread_feat()

    attend(3)
    push("po", po, ro, partner)
    push("pml", pml, rml, partner)

    z_send = []
    for n in range(4):
        short_send[SHORT - 1, n].wait_recv()
        long_send[LONG - 1, n].wait_recv()
        rl[LONG - 1, n] = rl[LONG - 1, n] + rs[SHORT - 1, n] + xbuf[quarters[n], y]
        if n < 3:
            z_send.append(push("z", rl.at[LONG - 1, n], zr.at[n], z_peers[n], z_r.at[n]))

    for j in range(NY - 1):
        push("by", bias_chip, bias_y.at[j], y_peers[j])

    lane = lax.broadcasted_iota(jnp.int32, (ROWS, HD), 1)
    freq = jnp.exp(-((lane % 64).astype(F32) * (2.0 / HD)) * math.log(1000000.0))
    is_key = tp < NX
    for s in range(2):
        angle = (lenc[...] + float(s)) * freq
        sine = jnp.sin(angle)
        cosf[s] = jnp.where(is_key, jnp.cos(angle), 1.0)
        sinf[s] = jnp.where(is_key, jnp.where(lane < 64, -sine, sine), 0.0)

    total_w = rl[LONG - 1, 3]
    for j in range(NZ - 1):
        z_send[j].wait_recv()
        total_w = total_w + zr[j]
    wf[zh] = total_w
    zg = [push("zg", wf.at[zh], wf.at[zh], z_peers[j], zg_r.at[j]) for j in range(NZ - 1)]

    take("by", bias_y)
    total_bias = bias_chip[...]
    for j in range(NY - 1):
        total_bias = total_bias + bias_y[j]
    bias_row[...] = total_bias
    for j in range(NZ - 1):
        push("bz", bias_row, bias_z.at[j], z_peers[j])

    def entry(s, total, bias):
        total = total + bias
        turned = total * cosf[s] + pltpu.roll(total, 64, 1) * sinf[s]
        kvown[s] = turned.astype(BF16)
        push(f"e{s}", kvown.at[s], kvpeer.at[s], partner)

    def product(i, cc):
        rows = feat[i, :, cc].reshape(NY * ROWS, HD)
        return jnp.dot(rows, wf[i], preferred_element_type=F32)

    take("feat_x", feat.at[pl.ds(0, NX - 1)])
    part_sib[...] = product(zh, other_core)
    part_own[...] = product(zh, core)
    for j in range(NZ - 1):
        i = (zh - j - 1 + NZ) % NZ
        zg[j].wait_recv()
        part_sib[...] += product(i, other_core)
        if j == NZ - 2:
            push("part", part_sib, part_in, sibling)
        part_own[...] += product(i, core)
    take("part", part_in)
    part_own[...] += part_in[...]
    ring_out[...] = part_own[...].astype(BF16).reshape(NY, ROWS, HD)
    for j in range(1, NY):
        push("ring", ring_out.at[(y + j) % NY], ring_in.at[j - 1], y_peers[j - 1])

    h_copy.wait()
    take("hx", hf.at[pl.ds(0, 2 * (NX - 1))])
    total = jnp.zeros((ROWS, HD), F32)
    for t in range(8):
        total = total + jnp.dot(
            hf[t], wv[t].reshape(STRIP, HD), preferred_element_type=F32)
    entry(0, total, bias_ref[...].astype(F32))

    def add_entry(s, i, query, key, value):
        score = jnp.sum(query * key, axis=1, keepdims=True)
        old = mo[i]
        peak = jnp.maximum(old, score)
        keep = jnp.exp2((old - peak) * SCALE2)
        weight = jnp.exp2((score - peak) * SCALE2)
        return (
            peak,
            lo[i] * keep + weight,
            oo[i] * keep + weight.astype(BF16).astype(F32) * value,
        )

    def new_pair(s):
        own, other = kvown[s].astype(F32), kvpeer[s].astype(F32)
        return jnp.where(is_key, own, other), jnp.where(is_key, other, own)

    take("po", ro)
    take("pml", rml)
    take("e0", kvpeer.at[0])
    key, value = new_pair(0)
    for i in range(8):
        m2 = rml[:, i:i + 1]
        l2 = rml[:, 8 + i:9 + i]
        m1 = mo[i]
        peak = jnp.maximum(m1, m2)
        e1 = jnp.exp2((m1 - peak) * SCALE2)
        e2 = jnp.exp2((m2 - peak) * SCALE2)
        mo[i] = peak
        lo[i] = lo[i] * e1 + l2 * e2
        oo[i] = oo[i] * e1 + ro[i].astype(F32) * e2
        query = qo[i // 4, :, pl.ds(i % 4 * HD, HD)].astype(F32)
        m, l, o = add_entry(0, i, query, key, value)
        if i < 4:
            out_ref[0, :, pl.ds(i * HD, HD)] = (o / l).astype(BF16)
        else:
            mo[i], lo[i], oo[i] = m, l, o
    take("bz", bias_z)
    fresh_bias = bias_row[...].astype(F32)
    for j in range(NZ - 1):
        fresh_bias = fresh_bias + bias_z[j].astype(F32)

    sent("die", xbuf)
    sent("long", rl)
    sent("short", rs)
    sent("z", zr)
    sent("zg", zr)
    sent("hz", hf.at[0])
    sent("hx", hf.at[pl.ds(0, 2 * (NX - 1))])
    sent("feat_x", feat.at[pl.ds(0, NX - 1)])
    sent("q", qp)
    sent("po", po)
    sent("pml", pml)
    sent("bd", bias_die)
    sent("by", bias_y)
    sent("bz", bias_z)
    sent("part", part_sib)
    sent("e0", kvown.at[0])
    sent("feat_y", ring_in)

    @pl.when(lead)
    def _():
        sent("feat_z", feat.at[0])

    @pl.when(jnp.logical_not(lead))
    def _():
        sent("feat_die", kvown.at[0])

    own_rows = pl.ds(pl.multiple_of(y * ROWS, ROWS), ROWS)
    total = part_own[own_rows]
    take("ring", ring_in)
    for j in range(NY - 1):
        total = total + ring_in[j].astype(F32)
    entry(1, total, fresh_bias[:1])
    sent("ring", ring_in)

    take("e1", kvpeer.at[1])
    key, value = new_pair(1)
    for i in range(4, 8):
        query = qo[1, :, pl.ds((i - 4) * HD, HD)].astype(F32)
        m, l, o = add_entry(1, i, query, key, value)
        out_ref[1, :, pl.ds((i - 4) * HD, HD)] = (o / l).astype(BF16)
    sent("e1", kvown.at[1])


def on_device(hidden, queries, kv_cache, lengths, weights, kv_bias, owner_group):
    sem = pltpu.SemaphoreType.DMA
    vmem = pltpu.VMEM
    any_spec = pl.BlockSpec(memory_space=pl.ANY)
    vmem_spec = pl.BlockSpec(memory_space=pltpu.VMEM)
    wide = (8, ROWS, HD)
    scratch = [
        vmem((1, ROWS), jnp.int32), vmem((1, HD), BF16), pltpu.SMEM((1,), jnp.int32),
        vmem((8, NY, HD, HD), BF16), vmem((4, NY, HD, HD), BF16),
        vmem((LONG, 4, HD, HD), BF16), vmem((SHORT, 4, HD, HD), BF16),
        vmem((NZ - 1, HD, HD), BF16), vmem((4, HD, HD), BF16),
        vmem((NX, NY, 2, ROWS, HD), BF16),
        vmem((8, ROWS, STRIP), BF16), vmem((ROWS * 64, 256), BF16),
        vmem((2, ROWS, 512), BF16), vmem((2, ROWS, 512), BF16),
        vmem(wide, F32), vmem(wide, F32), vmem(wide, F32),
        vmem(wide, BF16), vmem((ROWS, HD), F32),
        vmem(wide, BF16), vmem((ROWS, HD), F32),
        vmem((ROWS, HD), F32), vmem((2, ROWS, HD), F32), vmem((2, ROWS, HD), F32),
        vmem((16, HD), BF16), vmem((16, HD), BF16), vmem((16, HD), BF16),
        vmem((NY - 1, 16, HD), BF16), vmem((16, HD), BF16), vmem((NZ - 1, 16, HD), BF16),
        vmem((NY * ROWS, HD), F32), vmem((NY * ROWS, HD), F32), vmem((NY * ROWS, HD), F32),
        vmem(wide, BF16), vmem((NY - 1, ROWS, HD), BF16),
        vmem((2, ROWS, HD), BF16), vmem((2, ROWS, HD), BF16),
        sem((8,)), sem((NY,)), sem((LONG, 4)), sem((SHORT, 4)),
        sem((3,)), sem((3,)), sem((21,)), sem((21,)),
    ]
    return pl.pallas_call(
        kernel,
        out_shape=pltpu.VMEM((2, ROWS, 512), BF16),
        in_specs=[any_spec] * 7,
        out_specs=vmem_spec,
        scratch_shapes=scratch,
        compiler_params=pltpu.CompilerParams(
            collective_id=0, has_side_effects=True, vmem_limit_bytes=56 << 20),
    )(
        weights.reshape(8, NY, HD, HD), kv_cache.reshape(ROWS * 64, 256), hidden,
        queries.reshape(2, ROWS, 512), lengths.reshape(1, ROWS), kv_bias,
        owner_group,
    )


def solution(mesh):
    in_specs = (
        P(None, "group", "tp"),
        P(None, "group", "tp", None),
        P("group", "tp", None, None),
        P("group"),
        P("group", None, "tp"),
        P("group", "tp"),
        P(),
    )
    out_specs = P(None, "group", "tp")
    return jax.shard_map(
        on_device, mesh=mesh, in_specs=in_specs, out_specs=out_specs, check_vma=False
    )
```
